256 devices in a mesh: job: 32 (over x, y, core), seq: 8 (over z).
Axes of the slice: x: 4, y: 4, z: 8, core: 2. Of those that a mesh axis runs over, the one named last changes fastest.
Arguments:
- text_cache: bfloat16 [32, 2, 512, 4096], P('job', None, 'seq'), may hold values from -6 to 6
- source: int32 [32], replicated, may hold values from 0 to 63, as said below
- text_len: int32 [32], replicated, may hold values from 1 to 512, as said below
- query: bfloat16 [32, 2048, 3072], P('job', 'seq'), may hold values from -64 to 64
- w_text: bfloat16 [4096, 5120], P('job', 'seq'), may hold values from -0.09375 to 0.09375
- b_text: bfloat16 [5120], P('seq'), may hold values from -3 to 3
- w_key: bfloat16 [5120, 3072], P('job', 'seq'), may hold values from -0.078125 to 0.078125
- w_value: bfloat16 [5120, 3072], P('job', 'seq'), may hold values from -0.078125 to 0.078125
- b_value: bfloat16 [3072], P('seq'), may hold values from -3 to 3
Outputs:
- attended: bfloat16 [32, 2048, 3072], P('job', 'seq')
The draws below stay inside these ranges and needn't reach their ends.
Inputs may be any that keep to these rules, and one draw needn't show every extreme that they name: `source`: entries are distinct flat cache indices; 0 and 63 occur in every draw. `text_len`: some group has 512 live text tokens and some has 1.
All inputs are finite; a program needn't handle non-finite values.
Results may differ from the reference program's by a relative error of at most 0.008.
Values may be sent and summed in bfloat16 or wider, within the bound.
A program may use at most 128 MiB of HBM per device.

```python
import jax
import jax.numpy as jnp
from jax import lax

DM = 5120
DT = 4096
TXT = 512
HD = 128
HEADS = 24
SLOTS = 2
HQ = 3072
VIDEO = 2048
N_JOB = 32


def draw_source(key, part):
    first_key = jax.random.fold_in(key, 11)
    second_key = jax.random.fold_in(key, 12)
    total = N_JOB * SLOTS
    inner = jax.random.permutation(first_key, total - 2) + 1
    chosen = jnp.concatenate([jnp.zeros((1,), jnp.int32), inner[:N_JOB - 2].astype(jnp.int32), jnp.full((1,), total - 1, jnp.int32)])
    return jax.random.permutation(second_key, chosen).astype(jnp.int32)


def draw_text_len(key, part):
    first_key = jax.random.fold_in(key, 21)
    second_key = jax.random.fold_in(key, 22)
    lengths = jax.random.randint(first_key, (N_JOB,), 1, TXT + 1).astype(jnp.int32)
    longest = jax.random.randint(second_key, (), 0, N_JOB).astype(jnp.int32)
    lengths = lengths.at[longest].set(TXT)
    lengths = lengths.at[(longest + 1) % N_JOB].set(1)
    return lengths.astype(jnp.int32)


def draw_query(key, part):
    first_key = jax.random.fold_in(key, 31)
    shape = (N_JOB, VIDEO, HQ)
    values = jnp.clip(2.0 * jax.random.normal(first_key, shape, jnp.float32), -16.0, 16.0)
    return values.astype(jnp.bfloat16)


def block_scale(stream_key, extent, shards, low, largest):
    gain = 1.0
    for axis_at, blocks in shards:
        heights = jax.random.uniform(jax.random.fold_in(jax.random.fold_in(stream_key, 6), axis_at), (blocks,), jnp.float32, low / len(shards), largest / len(shards))
        gain = gain * jnp.repeat(jnp.exp(heights), extent[axis_at] // blocks).reshape((-1,) + (1,) * (len(extent) - 1 - axis_at))
    return gain


def bell_draw(key, dims, scale, reach, split=(), held_as=jnp.bfloat16):
    result = jax.random.normal(key, dims, jnp.float32) * scale
    if len(split) > 0:
        result = block_scale(key, dims, split, -0.22, 0.18) * result
    return jnp.clip(result, min=-reach, max=reach).astype(held_as)


def setup_inputs(seed: int = 0) -> dict:
    key_list = jax.random.split(jax.random.key(seed), 10)
    return {
        "text_cache": bell_draw(key_list[0], (N_JOB, SLOTS, TXT, DT), 1.0, 6.0, ((0, 32), (2, 8))),
        "source": draw_source(jax.random.fold_in(key_list[9], 71), 0),
        "text_len": draw_text_len(jax.random.fold_in(key_list[9], 71), 0),
        "query": draw_query(jax.random.fold_in(key_list[9], 71), 0),
        "w_text": bell_draw(key_list[4], (DT, DM), DT ** -0.5, 0.09375, ((0, 32), (1, 8))),
        "b_text": bell_draw(key_list[5], (DM,), 0.5, 3.0, ((0, 8),)),
        "w_key": bell_draw(key_list[6], (DM, HQ), DM ** -0.5, 0.078125, ((0, 32), (1, 8))),
        "w_value": bell_draw(key_list[7], (DM, HQ), DM ** -0.5, 0.078125, ((0, 32), (1, 8))),
        "b_value": bell_draw(key_list[8], (HQ,), 0.5, 3.0, ((0, 8),)),
    }


def attend(queries, keys, values, key_live):
    score_scale = HD ** -0.5
    scores = jnp.einsum("rhd,khd->hrk", queries.astype(jnp.float32), keys.astype(jnp.float32)) * score_scale
    scores = jnp.where(key_live[None, None, :], scores, jnp.float32(-1e30))
    row_peak = jnp.max(scores, axis=-1, keepdims=True)
    exponent = jnp.exp(scores - row_peak)
    probabilities = (exponent / jnp.sum(exponent, axis=-1, keepdims=True)).astype(jnp.bfloat16)
    mixed = jnp.einsum("hrk,khd->rhd", probabilities.astype(jnp.float32), values.astype(jnp.float32))
    return mixed.astype(jnp.bfloat16).reshape(queries.shape[0], -1)


def reference(text_cache, source, text_len, query, w_text, b_text, w_key, w_value, b_value):
    flat_cache = text_cache.reshape(N_JOB * SLOTS, TXT, DT)

    def per_job(items):
        cache_index, length, queries = items
        text_rows = lax.dynamic_index_in_dim(flat_cache, cache_index, 0, keepdims=False)
        preact = jnp.dot(text_rows, w_text, preferred_element_type=jnp.float32) + b_text.astype(jnp.float32)
        hidden = jax.nn.gelu(preact, approximate=True).astype(jnp.bfloat16)
        keys = jnp.dot(hidden, w_key, preferred_element_type=jnp.float32).astype(jnp.bfloat16)
        values = (jnp.dot(hidden, w_value, preferred_element_type=jnp.float32) + b_value.astype(jnp.float32)).astype(jnp.bfloat16)
        key_live = jnp.arange(TXT) < length
        return attend(queries.reshape(VIDEO, HEADS, HD), keys.reshape(TXT, HEADS, HD), values.reshape(TXT, HEADS, HD), key_live)

    return lax.map(per_job, (source, text_len, query))
```

```python
import functools

import jax
import jax.numpy as jnp
from jax import lax
from jax.experimental import pallas as pl
from jax.experimental.pallas import tpu as pltpu
from jax.sharding import PartitionSpec as P

MESH = pl.DeviceIdType.MESH
HD = 128
NJ, NZ, NX = 32, 8, 4
TXT, DT, DM, HQ, VR = 512, 4096, 5120, 3072, 256
ROWS = TXT // NZ
HB, KB = DM // NZ, HQ // NZ
WIN = 256
DEPTHS = (DT // NJ, DM // NJ, DM // NJ)
N_SEND = 224


def kernel(
    cache, source, text_len, query, w_text, w_key, w_value, bias, out_hbm,
    slabs, picked, txt, wt, wk, wv, hid, kall, vall, prob, qv, ov, bias_far, acc,
    send_sem, route_send, route_recv, local_sem, start_recv, flow_recv, twin_recv,
    text_recv, hid_recv, key_recv, value_recv, bias_recv, query_sem,
):
    me, z = lax.axis_index("job"), lax.axis_index("seq")
    core, chip = lax.rem(me, 2), me // 2
    x, y = chip // NX, lax.rem(chip, NX)
    u, v = jnp.where(core == 0, x, y), jnp.where(core == 0, y, x)
    step_u, step_v = 8 - 6 * core, 2 + 6 * core
    up, down, far = lax.rem(z + 1, NZ), lax.rem(z + NZ - 1, NZ), lax.rem(z + 4, NZ)
    twin = me + 1 - 2 * core

    def block(h):
        return z if h == 0 else far

    def at_uv(a, b):
        return lax.rem(u + a + NX, NX) * step_u + lax.rem(v + b + NX, NX) * step_v

    pending = []

    def send(src, dst, recv, job, seq):
        n = len(pending)
        copy = pltpu.make_async_remote_copy(
            src_ref=src, dst_ref=dst, send_sem=send_sem.at[n], recv_sem=recv,
            device_id={"job": job, "seq": seq}, device_id_type=MESH,
        )
        copy.start()
        pending.append(copy)

    def arrive(ref, sem):
        pltpu.make_async_copy(ref, ref, sem).wait()

    barrier = pltpu.get_barrier_semaphore()

    def greet(job, seq):
        pl.semaphore_signal(barrier, inc=1, device_id={"job": job, "seq": seq}, device_id_type=MESH)

    @pl.loop(1, NJ)
    def _(i):
        greet(lax.rem(me + i, NJ), z)

    greet(me, up)
    greet(me, down)
    greet(me, far)
    greet(twin, far)
    pl.semaphore_wait(barrier, NJ - 1 + 4)

    def slab_copy(i):
        to = lax.rem(me + i, NJ)
        return pltpu.make_async_remote_copy(
            src_ref=cache.at[0, :, :, pl.ds(pl.multiple_of(to * 128, 128), 128)],
            dst_ref=slabs.at[pl.ds(2 * me, 2)],
            send_sem=route_send.at[0, i], recv_sem=route_recv.at[0],
            device_id={"job": to, "seq": z}, device_id_type=MESH,
        )

    @pl.loop(1, NJ)
    def _(i):
        slab_copy(i).start()

    my_columns = pl.ds(pl.multiple_of(me * 128, 128), 128)
    own_slab = pltpu.make_async_copy(
        cache.at[0, :, :, my_columns], slabs.at[pl.ds(2 * me, 2)], local_sem.at[0]
    )
    own_slab.start()

    weights = ((w_text, wt), (w_key, wk), (w_value, wv))
    first = []
    for t, (shard, whole) in enumerate(weights):
        n = DEPTHS[t]
        rows = pl.ds(pl.multiple_of(me * n, 32), n)
        keep = pltpu.make_async_copy(shard, whole.at[0, rows], start_recv.at[t, 0])
        give = pltpu.make_async_remote_copy(
            src_ref=shard, dst_ref=whole.at[0, rows], send_sem=local_sem.at[1 + t],
            recv_sem=start_recv.at[t, 1], device_id={"job": twin, "seq": z}, device_id_type=MESH,
        )
        pl.when(core == 0)(keep.start)
        pl.when(core == 1)(give.start)
        first.append(give)
        send(shard, whole.at[1, rows], start_recv.at[t, core], chip * 2 + 1, far)
    send(bias, bias_far, bias_recv.at[0], me, far)
    fetch = [
        pltpu.make_async_copy(query.at[0, :, pl.ds(b * KB, KB)], qv.at[b], query_sem.at[b])
        for b in range(NZ)
    ]
    for copy in fetch:
        copy.start()

    def piece(t, a, b, part=None):
        n = 2 * DEPTHS[t]
        base = (lax.rem(u + a + NX, NX) * (step_u // 2) + lax.rem(v + b + NX, NX) * (step_v // 2)) * n
        if part is None:
            return weights[t][1].at[core, pl.ds(pl.multiple_of(base, 32), n)]
        base = base + part * (n // 2)
        return weights[t][1].at[core, pl.ds(pl.multiple_of(base, 32), n // 2)]

    def give(t, a, b, da, db, slot, part=None):
        ref = piece(t, a, b, part)
        send(ref, ref, flow_recv.at[t, slot], at_uv(da, db) + core, z)

    def share(t, a, b):
        ref = piece(t, a, b)
        send(ref, ref, twin_recv.at[t], twin, z)

    def across(t, a, index):
        give(t, a, 0, 0, 1, 4 + 4 * index)
        give(t, a, 0, 0, -1, 5 + 4 * index)
        share(t, a, 0)

    def flow_own(t):
        arrive(weights[t][0], start_recv.at[t, 0])
        arrive(weights[t][0], start_recv.at[t, 1])
        give(t, 0, 0, 1, 0, 0)
        give(t, 0, 0, -1, 0, 1)
        across(t, 0, 0)

    def flow_near(t):
        arrive(piece(t, -1, 0), flow_recv.at[t, 0])
        give(t, -1, 0, 1, 0, 2, 0)
        across(t, -1, 1)
        arrive(piece(t, 1, 0), flow_recv.at[t, 1])
        give(t, 1, 0, -1, 0, 3, 1)
        across(t, 1, 2)

    def flow_far(t):
        arrive(piece(t, 2, 0, 0), flow_recv.at[t, 2])
        arrive(piece(t, 2, 0, 1), flow_recv.at[t, 3])
        across(t, 2, 3)

    PLACES = (0, -1, 1, 2)

    def flow_second(t, index):
        a = PLACES[index]
        arrive(piece(t, a, -1), flow_recv.at[t, 4 + 4 * index])
        give(t, a, -1, 0, 1, 6 + 4 * index, 0)
        share(t, a, -1)
        arrive(piece(t, a, 1), flow_recv.at[t, 5 + 4 * index])
        give(t, a, 1, 0, -1, 7 + 4 * index, 1)
        share(t, a, 1)

    def flow_last(t, index):
        a = PLACES[index]
        arrive(piece(t, a, 2, 0), flow_recv.at[t, 6 + 4 * index])
        arrive(piece(t, a, 2, 1), flow_recv.at[t, 7 + 4 * index])
        share(t, a, 2)

    def flow_twin(t):
        arrive(weights[t][1].at[1 - core], twin_recv.at[t])

    flow_own(0)

    own_slab.wait()
    arrive(slabs.at[pl.ds(0, 2 * (NJ - 1))], route_recv.at[0])

    @pl.loop(0, NJ)
    def _(g):
        picked[g] = slabs[source[g]]

    mine = slice(96, 96 + ROWS)

    def job_copy(i):
        to = lax.rem(me + i, NJ)
        return pltpu.make_async_remote_copy(
            src_ref=picked.at[to], dst_ref=txt.at[mine, my_columns],
            send_sem=route_send.at[1, i], recv_sem=route_recv.at[1],
            device_id={"job": to, "seq": z}, device_id_type=MESH,
        )

    @pl.loop(1, NJ)
    def _(i):
        job_copy(i).start()

    own_job = pltpu.make_async_copy(picked.at[me], txt.at[mine, my_columns], local_sem.at[0])
    own_job.start()

    flow_near(0)

    own_job.wait()
    arrive(picked.at[pl.ds(0, NJ - 1)], route_recv.at[1])
    halves = (slice(0, DT // 2), slice(DT // 2, DT))
    for p, cols in enumerate(halves):
        send(txt.at[96:160, cols], txt.at[32:96, cols], text_recv.at[p, 0], me, up)
        send(txt.at[96:160, cols], txt.at[160:224, cols], text_recv.at[p, 1], me, down)
    flow_far(0)
    flow_second(0, 0)
    for p, cols in enumerate(halves):
        arrive(txt.at[32:96, cols], text_recv.at[p, 0])
        send(txt.at[64:96, cols], txt.at[0:32, cols], text_recv.at[p, 2], me, up)
        arrive(txt.at[160:224, cols], text_recv.at[p, 1])
        send(txt.at[160:192, cols], txt.at[224:256, cols], text_recv.at[p, 3], me, down)
    flow_second(0, 1)
    flow_second(0, 2)
    flow_second(0, 3)
    flow_own(1)
    for index in range(4):
        flow_last(0, index)
    for p, cols in enumerate(halves):
        arrive(txt.at[0:32, cols], text_recv.at[p, 2])
        arrive(txt.at[224:256, cols], text_recv.at[p, 3])
    arrive(bias_far, bias_recv.at[0])
    flow_twin(0)

    def chunk(b, k):
        return hid.at[b, k * ROWS : (k + 1) * ROWS]

    def hid_send(b, k, way, hop, h):
        send(chunk(b, k), chunk(b, k - way), hid_recv.at[h, 0 if way == 1 else 1, hop, k], me, up if way == 1 else down)

    def hid_wait(b, k, way, hop, h):
        arrive(chunk(b, k - way), hid_recv.at[h, 0 if way == 1 else 1, hop, k])

    for h in range(2):
        acc[...] = jnp.zeros_like(acc)

        @pl.loop(0, 4)
        def _(i):
            at = pl.ds(pl.multiple_of(i * 1024, 1024), 1024)
            acc[...] += jnp.dot(txt[:, at], wt[h, at, :], preferred_element_type=jnp.float32)

        beside = (bias if h == 0 else bias_far)[0:1, 0:HB].astype(jnp.float32)
        for r in range(4):
            rows = slice(r * ROWS, (r + 1) * ROWS)
            hid[block(h), rows, :] = jax.nn.gelu(acc[rows, :] + beside, approximate=True).astype(jnp.bfloat16)
        for k in (3, 2, 1):
            hid_send(block(h), k, 1, 0, h)
            hid_send(block(h), 3 - k, -1, 0, h)

    def before(h, way, hop):
        return lax.rem(block(h) - way * hop + NZ, NZ)

    flow_near(1)
    for hop in (1, 2, 3):
        for h in range(2):
            for k in range(3, 0, -1):
                if k < hop:
                    continue
                for way in (1, -1):
                    src = (k - hop + 1) if way == 1 else 3 - (k - hop + 1)
                    b = before(h, way, hop)
                    hid_wait(b, src, way, hop - 1, h)
                    if k > hop:
                        hid_send(b, src - way, way, hop, h)
        if hop == 1:
            flow_far(1)
            flow_second(1, 0)
        if hop == 2:
            flow_second(1, 1)
            flow_second(1, 2)
            flow_second(1, 3)
            flow_own(2)
    for index in range(4):
        flow_last(1, index)
    flow_twin(1)
    flow_near(2)

    def project(whole, h, target, with_bias):
        acc[:, 0:KB] = jnp.zeros((WIN, KB), jnp.float32)

        @pl.loop(0, NZ)
        def _(b):
            at = pl.ds(pl.multiple_of(b * HB, 128), HB)
            acc[:, 0:KB] += jnp.dot(hid[b], whole[h, at, :], preferred_element_type=jnp.float32)

        total = acc[:, 0:KB]
        if with_bias:
            total = total + (bias if h == 0 else bias_far)[0:1, HB : HB + KB].astype(jnp.float32)
        target[z, h] = total.astype(jnp.bfloat16)

    def ring_send(target, sems, s, h):
        for way in (0, 1):
            if s < (4 if way == h else 3):
                origin = lax.rem(z + (NZ - s if way == 0 else s), NZ)
                ref = target.at[origin, h]
                send(ref, ref, sems.at[way, s, h], me, up if way == 0 else down)

    def ring_wait(target, sems, s, h):
        for way in (0, 1):
            if s <= (4 if way == h else 3):
                origin = lax.rem(z + (NZ - s if way == 0 else s), NZ)
                arrive(target.at[origin, h], sems.at[way, s - 1, h])

    def ring_step(target, sems, s):
        for h in range(2):
            ring_wait(target, sems, s, h)
            if s < 4:
                ring_send(target, sems, s, h)

    for h in range(2):
        project(wk, h, kall, False)
        ring_send(kall, key_recv, 0, h)
    flow_far(2)
    flow_second(2, 0)
    ring_step(kall, key_recv, 1)
    flow_second(2, 1)
    flow_second(2, 2)
    flow_second(2, 3)
    ring_step(kall, key_recv, 2)
    for index in range(4):
        flow_last(2, index)
    ring_step(kall, key_recv, 3)
    flow_twin(2)
    for h in range(2):
        project(wv, h, vall, True)
        ring_send(vall, value_recv, 0, h)
    ring_step(kall, key_recv, 4)
    for copy in fetch:
        copy.wait()

    live = text_len[me]
    scale = HD ** (-0.5)

    def dead(origin):
        at = lax.broadcasted_iota(jnp.int32, (1, WIN), 1) + (ROWS * origin - 96)
        at = jnp.where(at < 0, at + TXT, jnp.where(at >= TXT, at - TXT, at))
        return jnp.where(at < live, jnp.float32(0), jnp.float32(-1e30))

    NT = (((1,), (1,)), ((), ()))

    def weigh(q):
        @pl.loop(0, 2)
        def _(n):
            b = lax.rem(q + 4 * n, NZ)
            other = lax.rem(b + 4, NZ)
            off_a, off_b = dead(b), dead(other)
            for i in range(KB // HD):
                cols = slice(i * HD, (i + 1) * HD)
                ahead = qv[b, :, cols]
                sa = lax.dot_general(ahead, kall[b, 0, :, cols], NT, preferred_element_type=jnp.float32) * scale + off_a
                sb = lax.dot_general(ahead, kall[other, 1, :, cols], NT, preferred_element_type=jnp.float32) * scale + off_b
                peak = jnp.maximum(jnp.max(sa, axis=1, keepdims=True), jnp.max(sb, axis=1, keepdims=True))
                ea, eb = jnp.exp(sa - peak), jnp.exp(sb - peak)
                share_of = 1.0 / (jnp.sum(ea, axis=1, keepdims=True) + jnp.sum(eb, axis=1, keepdims=True))
                prob[b, i, :, 0:WIN] = (ea * share_of).astype(jnp.bfloat16)
                prob[b, i, :, WIN:TXT] = (eb * share_of).astype(jnp.bfloat16)

    def mix(q):
        @pl.loop(0, 2)
        def _(n):
            b = lax.rem(q + 4 * n, NZ)
            other = lax.rem(b + 4, NZ)
            for i in range(KB // HD):
                cols = slice(i * HD, (i + 1) * HD)
                total = jnp.dot(prob[b, i, :, 0:WIN], vall[b, 0, :, cols], preferred_element_type=jnp.float32)
                total += jnp.dot(prob[b, i, :, WIN:TXT], vall[other, 1, :, cols], preferred_element_type=jnp.float32)
                ov[b, :, cols] = total.astype(jnp.bfloat16)

    def quarter(d):
        return lax.rem(z + d, 4)

    weigh(quarter(2))
    ring_step(vall, value_recv, 1)
    weigh(quarter(1))
    ring_step(vall, value_recv, 2)
    weigh(quarter(3))
    weigh(quarter(0))
    ring_step(vall, value_recv, 3)
    mix(quarter(2))
    mix(quarter(1))
    mix(quarter(3))
    ring_step(vall, value_recv, 4)
    mix(quarter(0))
    store = [
        pltpu.make_async_copy(ov.at[b], out_hbm.at[0, :, pl.ds(b * KB, KB)], query_sem.at[b])
        for b in range(NZ)
    ]
    for copy in store:
        copy.start()
    for copy in store:
        copy.wait()

    for copy in pending:
        copy.wait_send()
    for copy in first:
        pl.when(core == 1)(copy.wait_send)

    @pl.loop(1, NJ)
    def _(i):
        slab_copy(i).wait_send()
        job_copy(i).wait_send()


def body(text_cache, source, text_len, query, w_text, b_text, w_key, w_value, b_value):
    bf16, dma = jnp.bfloat16, pltpu.SemaphoreType.DMA
    bias = jnp.broadcast_to(jnp.concatenate([b_text, b_value])[None], (16, HB + KB))
    whole, smem, vmem = (pl.BlockSpec(memory_space=s) for s in (pl.ANY, pltpu.SMEM, pltpu.VMEM))
    return pl.pallas_call(
        kernel,
        out_shape=jax.ShapeDtypeStruct((1, VR, HQ), bf16),
        in_specs=[whole, smem, smem, whole, whole, whole, whole, vmem],
        out_specs=whole,
        scratch_shapes=[
            pltpu.VMEM((2 * NJ, ROWS, 128), bf16),
            pltpu.VMEM((NJ, ROWS, 128), bf16),
            pltpu.VMEM((WIN, DT), bf16),
            pltpu.VMEM((2, DT, HB), bf16),
            pltpu.VMEM((2, DM, KB), bf16),
            pltpu.VMEM((2, DM, KB), bf16),
            pltpu.VMEM((NZ, WIN, HB), bf16),
            pltpu.VMEM((NZ, 2, WIN, KB), bf16),
            pltpu.VMEM((NZ, 2, WIN, KB), bf16),
            pltpu.VMEM((NZ, KB // HD, VR, TXT), bf16),
            pltpu.VMEM((NZ, VR, KB), bf16),
            pltpu.VMEM((NZ, VR, KB), bf16),
            pltpu.VMEM((16, HB + KB), bf16),
            pltpu.VMEM((WIN, HB), jnp.float32),
            dma((N_SEND,)),
            dma((2, NJ)),
            dma((2,)),
            dma((4,)),
            dma((3, 2)),
            dma((3, 20)),
            dma((3,)),
            dma((2, 4)),
            dma((2, 2, 3, 4)),
            dma((2, 4, 2)),
            dma((2, 4, 2)),
            dma((1,)),
            dma((NZ,)),
        ],
        compiler_params=pltpu.CompilerParams(
            collective_id=0, has_side_effects=True, vmem_limit_bytes=60 * 2**20
        ),
    )(text_cache, source, text_len, query, w_text, w_key, w_value, bias)


def solution(mesh):
    in_specs = (
        P("job", None, "seq", None),
        P(),
        P(),
        P("job", "seq", None),
        P("job", "seq"),
        P("seq"),
        P("job", "seq"),
        P("job", "seq"),
        P("seq"),
    )
    out_specs = P("job", "seq", None)
    return jax.shard_map(body, mesh=mesh, in_specs=in_specs, out_specs=out_specs, check_vma=False)
```

```python
import functools

import jax
import jax.numpy as jnp
from jax import lax
from jax.experimental import pallas as pl
from jax.experimental.pallas import tpu as pltpu
from jax.sharding import PartitionSpec as P

MESH = pl.DeviceIdType.MESH
HD = 128
NJ, NZ, NX = 32, 8, 4
TXT, DT, DM, HQ, VR = 512, 4096, 5120, 3072, 256
ROWS = TXT // NZ
HB, KB = DM // NZ, HQ // NZ
WIN = 256
DEPTHS = (DT // NJ, DM // NJ, DM // NJ)
HALF = ROWS // 2
N_SEND = 320


def kernel(
    cache, source, text_len, query, w_text, w_key, w_value, b_text, b_value, out,
    slabs_a, slabs_b, picked, txt, wt, wk, wv, hid, kall, vall, prob, qv, bias, bias_far, acc,
    send_sem, route_send, route_recv, local_sem, start_recv, flow_recv, twin_recv,
    text_recv, hid_recv, key_recv, value_recv, bias_recv, query_sem,
):
    me, z = lax.axis_index("job"), lax.axis_index("seq")
    core, chip = lax.rem(me, 2), me // 2
    x, y = chip // NX, lax.rem(chip, NX)
    u, v = jnp.where(core == 0, x, y), jnp.where(core == 0, y, x)
    step_u, step_v = 8 - 6 * core, 2 + 6 * core
    up, down, far = lax.rem(z + 1, NZ), lax.rem(z + NZ - 1, NZ), lax.rem(z + 4, NZ)
    twin = me + 1 - 2 * core

    def block(h):
        return z if h == 0 else far

    def at_uv(a, b):
        return lax.rem(u + a + NX, NX) * step_u + lax.rem(v + b + NX, NX) * step_v

    pending = []

    def send(src, dst, recv, job, seq):
        n = len(pending)
        copy = pltpu.make_async_remote_copy(
            src_ref=src, dst_ref=dst, send_sem=send_sem.at[n], recv_sem=recv,
            device_id={"job": job, "seq": seq}, device_id_type=MESH,
        )
        copy.start()
        pending.append(copy)

    def arrive(ref, sem):
        pltpu.make_async_copy(ref, ref, sem).wait()

    barrier = pltpu.get_barrier_semaphore()

    def greet(job, seq):
        pl.semaphore_signal(barrier, inc=1, device_id={"job": job, "seq": seq}, device_id_type=MESH)

    @pl.loop(1, NJ)
    def _(i):
        greet(lax.rem(me + i, NJ), z)

    greet(me, up)
    greet(me, down)
    greet(me, far)
    greet(twin, far)
    pl.semaphore_wait(barrier, NJ - 1 + 4)

    slabs = (slabs_a, slabs_b)

    def slab_copy(p, i):
        to = lax.rem(me + i, NJ)
        return pltpu.make_async_remote_copy(
            src_ref=cache.at[0, :, p * HALF : (p + 1) * HALF, pl.ds(pl.multiple_of(to * 128, 128), 128)],
            dst_ref=slabs[p].at[pl.ds(2 * me, 2)],
            send_sem=route_send.at[0, p, i], recv_sem=route_recv.at[0, p],
            device_id={"job": to, "seq": z}, device_id_type=MESH,
        )

    my_columns = pl.ds(pl.multiple_of(me * 128, 128), 128)
    own_slab = [
        pltpu.make_async_copy(
            cache.at[0, :, p * HALF : (p + 1) * HALF, my_columns],
            slabs[p].at[pl.ds(2 * me, 2)],
            local_sem.at[p],
        )
        for p in range(2)
    ]
    for p in range(2):

        @pl.loop(1, NJ)
        def _(i):
            slab_copy(p, i).start()

        own_slab[p].start()

    weights = ((w_text, wt), (w_key, wk), (w_value, wv))
    keeps = [
        pltpu.make_async_copy(shard, whole.at[0, me], start_recv.at[t, 0])
        for t, (shard, whole) in enumerate(weights)
    ]
    for t, (shard, whole) in enumerate(weights):
        keeps[t].start()
        send(shard, whole.at[1, me], start_recv.at[t, 1], me, far)
    bias[:, 0:HB] = jnp.broadcast_to(b_text[...].astype(jnp.float32), (16, HB)).astype(jnp.bfloat16)
    bias[:, HB : HB + KB] = jnp.broadcast_to(b_value[...].astype(jnp.float32), (16, KB)).astype(jnp.bfloat16)
    send(bias, bias_far, bias_recv.at[0], me, far)
    fetch = [
        pltpu.make_async_copy(query.at[0, :, pl.ds(b * KB, KB)], qv.at[b], query_sem.at[b])
        for b in range(NZ)
    ]
    for copy in fetch:
        copy.start()

    def piece(t, h, a, b, part=None):
        ref = weights[t][1].at[h, at_uv(a, b) + core]
        if part is None:
            return ref
        n = DEPTHS[t] // 2
        return ref.at[pl.ds(part * n, n)]

    def give(t, h, a, b, da, db, slot, part=None):
        ref = piece(t, h, a, b, part)
        send(ref, ref, flow_recv.at[t, h, slot], at_uv(da, db) + core, z)

    def share(t, h, a, b):
        ref = piece(t, h, a, b)
        send(ref, ref, twin_recv.at[t, h], twin, z)

    def across(t, h, a, index):
        give(t, h, a, 0, 0, 1, 4 + 4 * index)
        give(t, h, a, 0, 0, -1, 5 + 4 * index)
        share(t, h, a, 0)

    def flow_own(t, h):
        arrive(weights[t][1].at[h, me], start_recv.at[t, h])
        give(t, h, 0, 0, 1, 0, 0)
        give(t, h, 0, 0, -1, 0, 1)
        across(t, h, 0, 0)

    def flow_near(t, h):
        arrive(piece(t, h, -1, 0), flow_recv.at[t, h, 0])
        give(t, h, -1, 0, 1, 0, 2, 0)
        across(t, h, -1, 1)
        arrive(piece(t, h, 1, 0), flow_recv.at[t, h, 1])
        give(t, h, 1, 0, -1, 0, 3, 1)
        across(t, h, 1, 2)

    def flow_far(t, h):
        arrive(piece(t, h, 2, 0, 0), flow_recv.at[t, h, 2])
        arrive(piece(t, h, 2, 0, 1), flow_recv.at[t, h, 3])
        across(t, h, 2, 3)

    PLACES = (0, -1, 1, 2)

    def flow_second(t, h, *indices):
        for index in indices:
            a = PLACES[index]
            arrive(piece(t, h, a, -1), flow_recv.at[t, h, 4 + 4 * index])
            give(t, h, a, -1, 0, 1, 6 + 4 * index, 0)
            share(t, h, a, -1)
            arrive(piece(t, h, a, 1), flow_recv.at[t, h, 5 + 4 * index])
            give(t, h, a, 1, 0, -1, 7 + 4 * index, 1)
            share(t, h, a, 1)

    def flow_last(t, h):
        for index, a in enumerate(PLACES):
            arrive(piece(t, h, a, 2, 0), flow_recv.at[t, h, 6 + 4 * index])
            arrive(piece(t, h, a, 2, 1), flow_recv.at[t, h, 7 + 4 * index])
            share(t, h, a, 2)

    def flow_twin(t, h):
        arrive(weights[t][1].at[h, 0 : NJ // 2], twin_recv.at[t, h])

    def first_row(p):
        return 96 + p * HALF

    def job_copy(p, i):
        to = lax.rem(me + i, NJ)
        return pltpu.make_async_remote_copy(
            src_ref=picked.at[p, to], dst_ref=txt.at[first_row(p) : first_row(p) + HALF, my_columns],
            send_sem=route_send.at[1, p, i], recv_sem=route_recv.at[1, p],
            device_id={"job": to, "seq": z}, device_id_type=MESH,
        )

    own_job = [
        pltpu.make_async_copy(
            picked.at[p, me], txt.at[first_row(p) : first_row(p) + HALF, my_columns], local_sem.at[p]
        )
        for p in range(2)
    ]

    def route_on(p):
        own_slab[p].wait()
        arrive(slabs[p].at[pl.ds(0, 2 * (NJ - 1))], route_recv.at[0, p])

        @pl.loop(0, NJ)
        def _(g):
            picked[p, g] = slabs[p][source[g]]

        @pl.loop(1, NJ)
        def _(i):
            job_copy(p, i).start()

        own_job[p].start()

    def lines(p, way, hops):
        at = first_row(p) - way * hops * ROWS
        return txt.at[at : at + HALF]

    def text_on(p):
        own_job[p].wait()
        arrive(picked.at[p, pl.ds(0, NJ - 1)], route_recv.at[1, p])
        for way in (2 * p - 1, 1 - 2 * p):
            send(lines(p, way, 0), lines(p, way, 1), text_recv.at[p, (1 + way) // 2], me, up if way == 1 else down)

    def text_pass(p):
        way = 2 * p - 1
        arrive(lines(p, way, 1), text_recv.at[p, (1 + way) // 2])
        send(lines(p, way, 1), lines(p, way, 2), text_recv.at[p, 2], me, up if way == 1 else down)

    def text_last(p):
        way = 2 * p - 1
        arrive(lines(p, -way, 1), text_recv.at[p, (1 - way) // 2])
        arrive(lines(p, way, 2), text_recv.at[p, 2])

    flow_own(0, 0)
    route_on(0)
    flow_near(0, 0)
    route_on(1)
    flow_own(0, 1)
    flow_far(0, 0)
    flow_second(0, 0, 0)
    text_on(0)
    flow_second(0, 0, 1, 2)
    flow_near(0, 1)
    text_on(1)
    text_pass(0)
    flow_second(0, 0, 3)
    flow_far(0, 1)
    flow_second(0, 1, 0)
    text_pass(1)
    flow_last(0, 0)
    flow_second(0, 1, 1, 2, 3)
    flow_own(1, 0)
    text_last(0)
    text_last(1)
    flow_twin(0, 0)

    def chunk(b, k):
        return hid.at[b, k * ROWS : (k + 1) * ROWS]

    def hid_send(b, k, way, hop, h):
        send(chunk(b, k), chunk(b, k - way), hid_recv.at[h, 0 if way == 1 else 1, hop, k], me, up if way == 1 else down)

    def hid_wait(b, k, way, hop, h):
        arrive(chunk(b, k - way), hid_recv.at[h, 0 if way == 1 else 1, hop, k])

    def embed(h):
        acc[...] = jnp.zeros_like(acc)

        @pl.loop(0, 4)
        def _(i):
            at = pl.ds(pl.multiple_of(i * 1024, 1024), 1024)
            part = wt[h, pl.ds(i * 8, 8)].reshape(1024, HB)
            acc[...] += jnp.dot(txt[:, at], part, preferred_element_type=jnp.float32)

        beside = (bias if h == 0 else bias_far)[0:1, 0:HB].astype(jnp.float32)
        for r in range(4):
            rows = slice(r * ROWS, (r + 1) * ROWS)
            hid[block(h), rows, :] = jax.nn.gelu(acc[rows, :] + beside, approximate=True).astype(jnp.bfloat16)
        for k in (3, 2, 1):
            hid_send(block(h), k, 1, 0, h)
            hid_send(block(h), 3 - k, -1, 0, h)

    def hid_pass(h, hop):
        for k in range(3, hop - 1, -1):
            for way in (1, -1):
                src = (k - hop + 1) if way == 1 else 3 - (k - hop + 1)
                b = lax.rem(block(h) - way * hop + NZ, NZ)
                hid_wait(b, src, way, hop - 1, h)
                if k > hop:
                    hid_send(b, src - way, way, hop, h)

    def project(whole, h, target, with_bias):
        acc[:, 0:KB] = jnp.zeros((WIN, KB), jnp.float32)

        @pl.loop(0, NZ)
        def _(b):
            part = whole[h, pl.ds(b * 4, 4)].reshape(HB, KB)
            acc[:, 0:KB] += jnp.dot(hid[b], part, preferred_element_type=jnp.float32)

        total = acc[:, 0:KB]
        if with_bias:
            total = total + (bias if h == 0 else bias_far)[0:1, HB : HB + KB].astype(jnp.float32)
        target[z, h] = total.astype(jnp.bfloat16)

    def ring_send(target, sems, s, h):
        for way in (0, 1):
            if s < (4 if way == h else 3):
                origin = lax.rem(z + (NZ - s if way == 0 else s), NZ)
                ref = target.at[origin, h]
                send(ref, ref, sems.at[way, s, h], me, up if way == 0 else down)

    def ring_wait(target, sems, s, h):
        for way in (0, 1):
            if s <= (4 if way == h else 3):
                origin = lax.rem(z + (NZ - s if way == 0 else s), NZ)
                arrive(target.at[origin, h], sems.at[way, s - 1, h])

    def ring_step(target, sems, s):
        for h in range(2):
            ring_wait(target, sems, s, h)
            if s < 4:
                ring_send(target, sems, s, h)

    embed(0)
    flow_last(0, 1)
    flow_near(1, 0)
    hid_pass(0, 1)
    flow_own(1, 1)
    flow_far(1, 0)
    flow_second(1, 0, 0)
    arrive(bias_far, bias_recv.at[0])
    flow_twin(0, 1)
    embed(1)
    hid_pass(0, 2)
    flow_second(1, 0, 1, 2)
    hid_pass(1, 1)
    flow_near(1, 1)
    hid_pass(0, 3)
    flow_second(1, 0, 3)
    hid_pass(1, 2)
    flow_far(1, 1)
    flow_second(1, 1, 0)
    hid_pass(1, 3)
    flow_last(1, 0)
    flow_second(1, 1, 1, 2, 3)
    flow_own(2, 0)
    flow_twin(1, 0)
    project(wk, 0, kall, False)
    ring_send(kall, key_recv, 0, 0)
    flow_last(1, 1)
    flow_near(2, 0)
    flow_own(2, 1)
    flow_twin(1, 1)
    project(wk, 1, kall, False)
    ring_send(kall, key_recv, 0, 1)
    flow_far(2, 0)
    flow_second(2, 0, 0)
    ring_step(kall, key_recv, 1)
    flow_second(2, 0, 1, 2)
    flow_near(2, 1)
    ring_step(kall, key_recv, 2)
    flow_second(2, 0, 3)
    flow_far(2, 1)
    flow_second(2, 1, 0)
    ring_step(kall, key_recv, 3)
    flow_last(2, 0)
    flow_second(2, 1, 1, 2, 3)
    flow_twin(2, 0)
    project(wv, 0, vall, True)
    ring_send(vall, value_recv, 0, 0)
    flow_last(2, 1)
    ring_step(kall, key_recv, 4)
    flow_twin(2, 1)
    project(wv, 1, vall, True)
    ring_send(vall, value_recv, 0, 1)
    for copy in fetch:
        copy.wait()

    live = text_len[me]
    scale = HD ** (-0.5)

    def dead(origin):
        at = lax.broadcasted_iota(jnp.int32, (1, WIN), 1) + (ROWS * origin - 96)
        at = jnp.where(at < 0, at + TXT, jnp.where(at >= TXT, at - TXT, at))
        return jnp.where(at < live, jnp.float32(0), jnp.float32(-1e30))

    NT = (((1,), (1,)), ((), ()))

    def weigh(q):
        @pl.loop(0, 2)
        def _(n):
            b = lax.rem(q + 4 * n, NZ)
            other = lax.rem(b + 4, NZ)
            off_a, off_b = dead(b), dead(other)
            for i in range(KB // HD):
                cols = slice(i * HD, (i + 1) * HD)
                ahead = qv[b, :, cols]
                sa = lax.dot_general(ahead, kall[b, 0, :, cols], NT, preferred_element_type=jnp.float32) * scale + off_a
                sb = lax.dot_general(ahead, kall[other, 1, :, cols], NT, preferred_element_type=jnp.float32) * scale + off_b
                peak = jnp.maximum(jnp.max(sa, axis=1, keepdims=True), jnp.max(sb, axis=1, keepdims=True))
                ea, eb = jnp.exp(sa - peak), jnp.exp(sb - peak)
                share_of = 1.0 / (jnp.sum(ea, axis=1, keepdims=True) + jnp.sum(eb, axis=1, keepdims=True))
                prob[b, i, :, 0:WIN] = (ea * share_of).astype(jnp.bfloat16)
                prob[b, i, :, WIN:TXT] = (eb * share_of).astype(jnp.bfloat16)

    def mix(q):
        @pl.loop(0, 2)
        def _(n):
            b = lax.rem(q + 4 * n, NZ)
            other = lax.rem(b + 4, NZ)
            for i in range(KB // HD):
                cols = slice(i * HD, (i + 1) * HD)
                total = jnp.dot(prob[b, i, :, 0:WIN], vall[b, 0, :, cols], preferred_element_type=jnp.float32)
                total += jnp.dot(prob[b, i, :, WIN:TXT], vall[other, 1, :, cols], preferred_element_type=jnp.float32)
                out[0, :, pl.ds(pl.multiple_of(b * KB + i * HD, HD), HD)] = total.astype(jnp.bfloat16)

    def quarter(d):
        return lax.rem(z + d, 4)

    weigh(quarter(2))
    ring_step(vall, value_recv, 1)
    weigh(quarter(1))
    ring_step(vall, value_recv, 2)
    weigh(quarter(3))
    weigh(quarter(0))
    ring_step(vall, value_recv, 3)
    mix(quarter(2))
    mix(quarter(1))
    mix(quarter(3))
    ring_step(vall, value_recv, 4)
    mix(quarter(0))

    for copy in pending:
        copy.wait_send()
    for p in range(2):

        @pl.loop(1, NJ)
        def _(i):
            slab_copy(p, i).wait_send()
            job_copy(p, i).wait_send()


def body(text_cache, source, text_len, query, w_text, b_text, w_key, w_value, b_value):
    bf16, dma = jnp.bfloat16, pltpu.SemaphoreType.DMA
    whole, smem, vmem = (pl.BlockSpec(memory_space=s) for s in (pl.ANY, pltpu.SMEM, pltpu.VMEM))
    return pl.pallas_call(
        kernel,
        out_shape=pltpu.VMEM((1, VR, HQ), bf16),
        in_specs=[whole, smem, smem, whole, whole, whole, whole, vmem, vmem],
        out_specs=vmem,
        scratch_shapes=[
            pltpu.VMEM((2 * NJ, HALF, 128), bf16),
            pltpu.VMEM((2 * NJ, HALF, 128), bf16),
            pltpu.VMEM((2, NJ, HALF, 128), bf16),
            pltpu.VMEM((WIN, DT), bf16),
            pltpu.VMEM((2, NJ, DT // NJ, HB), bf16),
            pltpu.VMEM((2, NJ, DM // NJ, KB), bf16),
            pltpu.VMEM((2, NJ, DM // NJ, KB), bf16),
            pltpu.VMEM((NZ, WIN, HB), bf16),
            pltpu.VMEM((NZ, 2, WIN, KB), bf16),
            pltpu.VMEM((NZ, 2, WIN, KB), bf16),
            pltpu.VMEM((NZ, KB // HD, VR, TXT), bf16),
            pltpu.VMEM((NZ, VR, KB), bf16),
            pltpu.VMEM((16, HB + KB), bf16),
            pltpu.VMEM((16, HB + KB), bf16),
            pltpu.VMEM((WIN, HB), jnp.float32),
            dma((N_SEND,)),
            dma((2, 2, NJ)),
            dma((2, 2)),
            dma((2,)),
            dma((3, 2)),
            dma((3, 2, 20)),
            dma((3, 2)),
            dma((2, 3)),
            dma((2, 2, 3, 4)),
            dma((2, 4, 2)),
            dma((2, 4, 2)),
            dma((1,)),
            dma((NZ,)),
        ],
        compiler_params=pltpu.CompilerParams(
            collective_id=0, has_side_effects=True, vmem_limit_bytes=56 * 2**20
        ),
    )(text_cache, source, text_len, query, w_text, w_key, w_value, b_text[None], b_value[None])


def solution(mesh):
    in_specs = (
        P("job", None, "seq", None),
        P(),
        P(),
        P("job", "seq", None),
        P("job", "seq"),
        P("seq"),
        P("job", "seq"),
        P("job", "seq"),
        P("seq"),
    )
    out_specs = P("job", "seq", None)
    return jax.shard_map(body, mesh=mesh, in_specs=in_specs, out_specs=out_specs, check_vma=False)
```

```python
import functools

import jax
import jax.numpy as jnp
from jax import lax
from jax.experimental import pallas as pl
from jax.experimental.pallas import tpu as pltpu
from jax.sharding import PartitionSpec as P

MESH = pl.DeviceIdType.MESH
HD = 128
NJ, NZ, NX = 32, 8, 4
TXT, DT, DM, HQ, VR = 512, 4096, 5120, 3072, 256
ROWS = TXT // NZ
HB, KB = DM // NZ, HQ // NZ
WIN = 256
DEPTHS = (DT // NJ, DM // NJ, DM // NJ)
HALF = ROWS // 2
N_SEND = 320
STEPS = (
    ("route_on", 0), ("own", 0, 0), ("route_on", 1), ("near", 0, 0, -1), ("near", 0, 0, 1), ("text_on", 0),
    ("second", 0, 0, 0, -1), ("second", 0, 0, 0, 1), ("own", 0, 1), ("second", 0, 0, 1, 1), ("text_on", 1),
    ("far", 0, 0), ("second", 0, 0, 1, -1), ("text_pass", 0), ("second", 0, 0, 2, 1), ("second", 0, 0, 2, -1),
    ("last", 0, 0, 0), ("near", 0, 1, 1), ("near", 0, 1, -1), ("second", 0, 1, 0, 1), ("second", 0, 1, 0, -1),
    ("text_pass", 1), ("second", 0, 0, 3, -1), ("second", 0, 0, 3, 1), ("last", 0, 0, 1), ("last", 0, 0, 2),
    ("second", 0, 1, 2, -1), ("second", 0, 1, 2, 1), ("far", 0, 1), ("second", 0, 1, 1, 1),
    ("second", 0, 1, 1, -1), ("last", 0, 1, 0), ("own", 1, 0), ("last", 0, 0, 3), ("last", 0, 1, 2),
    ("own", 1, 1), ("embed", 0), ("second", 0, 1, 3, -1), ("second", 0, 1, 3, 1), ("last", 0, 1, 1),
    ("near", 1, 0, -1), ("near", 1, 0, 1), ("second", 1, 0, 0, 1), ("second", 1, 0, 0, -1), ("near", 1, 1, 1),
    ("near", 1, 1, -1), ("second", 1, 1, 0, 1), ("second", 1, 1, 0, -1), ("hid", 0, 1, 3, 1),
    ("hid", 0, 1, 3, -1), ("last", 0, 1, 3), ("hid", 0, 1, 2, 1), ("hid", 0, 1, 2, -1),
    ("second", 1, 0, 1, 1), ("far", 1, 0), ("second", 1, 0, 1, -1), ("embed", 1), ("hid", 0, 2, 3, 1),
    ("hid", 0, 2, 3, -1), ("hid", 0, 1, 1, 1), ("hid", 0, 1, 1, -1), ("second", 1, 0, 2, -1),
    ("second", 1, 0, 2, 1), ("last", 1, 0, 0), ("second", 1, 1, 2, -1), ("second", 1, 1, 2, 1), ("far", 1, 1),
    ("hid", 0, 2, 2, 1), ("hid", 0, 2, 2, -1), ("second", 1, 1, 1, 1), ("second", 1, 1, 1, -1),
    ("last", 1, 1, 0), ("hid", 1, 1, 3, 1), ("hid", 1, 1, 3, -1), ("own", 2, 0), ("second", 1, 0, 3, -1),
    ("second", 1, 0, 3, 1), ("last", 1, 0, 1), ("last", 1, 0, 2), ("hid", 1, 1, 2, 1), ("hid", 1, 1, 2, -1),
    ("last", 1, 1, 2), ("own", 2, 1), ("hid", 1, 1, 1, 1), ("hid", 1, 1, 1, -1), ("second", 1, 1, 3, -1),
    ("second", 1, 1, 3, 1), ("last", 1, 1, 1), ("hid", 0, 3, 3, 1), ("hid", 0, 3, 3, -1), ("near", 2, 0, 1),
    ("near", 2, 0, -1), ("second", 2, 0, 0, 1), ("second", 2, 0, 0, -1), ("hid", 1, 2, 3, 1),
    ("hid", 1, 2, 3, -1), ("last", 1, 0, 3), ("hid", 1, 2, 2, 1), ("near", 2, 1, 1), ("hid", 1, 2, 2, -1),
    ("near", 2, 1, -1), ("second", 2, 1, 0, 1), ("second", 2, 1, 0, -1), ("last", 1, 1, 3),
    ("hid", 1, 3, 3, 1), ("hid", 1, 3, 3, -1), ("project", 1, 0), ("project", 1, 1), ("far", 2, 0),
    ("second", 2, 0, 1, -1), ("second", 2, 0, 1, 1), ("second", 2, 0, 2, -1), ("second", 2, 0, 2, 1),
    ("last", 2, 0, 0), ("second", 2, 1, 2, -1), ("second", 2, 1, 2, 1), ("far", 2, 1), ("second", 2, 1, 1, 1),
    ("second", 2, 1, 1, -1), ("last", 2, 1, 0), ("ring", 1, 1, 0, 0), ("ring", 1, 1, 0, 1),
    ("second", 2, 0, 3, 1), ("second", 2, 0, 3, -1), ("last", 2, 0, 1), ("last", 2, 0, 2), ("last", 2, 1, 2),
    ("second", 2, 1, 3, 1), ("second", 2, 1, 3, -1), ("ring", 1, 1, 1, 0), ("ring", 1, 1, 1, 1),
    ("last", 2, 1, 1), ("last", 2, 0, 3), ("last", 2, 1, 3), ("project", 2, 0), ("ring", 1, 2, 0, 0),
    ("ring", 1, 2, 0, 1), ("project", 2, 1), ("ring", 1, 2, 1, 0), ("ring", 1, 2, 1, 1), ("weigh", 2),
    ("ring", 2, 1, 0, 0), ("ring", 2, 1, 0, 1), ("ring", 1, 3, 0, 0), ("ring", 1, 3, 0, 1),
    ("ring", 2, 1, 1, 0), ("ring", 2, 1, 1, 1), ("ring", 1, 3, 1, 0), ("weigh", 1), ("ring", 1, 3, 1, 1),
    ("weigh", 3), ("ring", 2, 2, 0, 0), ("ring", 2, 2, 0, 1), ("ring", 1, 4, 0, 0), ("ring", 2, 2, 1, 1),
    ("ring", 2, 2, 1, 0), ("ring", 1, 4, 1, 1), ("mix", 2), ("weigh", 0), ("ring", 2, 3, 0, 0),
    ("ring", 2, 3, 0, 1), ("ring", 2, 3, 1, 0), ("mix", 1), ("ring", 2, 3, 1, 1), ("mix", 3),
    ("ring", 2, 4, 0, 0), ("ring", 2, 4, 1, 1), ("mix", 0),
)


def kernel(
    cache, source, text_len, query, w_text, w_key, w_value, b_text, b_value, out,
    slabs_a, slabs_b, picked, txt, wt, wk, wv, hid, kall, vall, prob, qv, bias, bias_far, acc,
    send_sem, route_send, route_recv, local_sem, start_recv, flow_recv, twin_recv,
    text_recv, hid_recv, key_recv, value_recv, bias_recv, query_sem,
):
    me, z = lax.axis_index("job"), lax.axis_index("seq")
    core, chip = lax.rem(me, 2), me // 2
    x, y = chip // NX, lax.rem(chip, NX)
    u, v = jnp.where(core == 0, x, y), jnp.where(core == 0, y, x)
    step_u, step_v = 8 - 6 * core, 2 + 6 * core
    up, down, far = lax.rem(z + 1, NZ), lax.rem(z + NZ - 1, NZ), lax.rem(z + 4, NZ)
    twin = me + 1 - 2 * core

    def block(h):
        return z if h == 0 else far

    def at_uv(a, b):
        return lax.rem(u + a + NX, NX) * step_u + lax.rem(v + b + NX, NX) * step_v

    pending = []

    def send(src, dst, recv, job, seq):
        n = len(pending)
        copy = pltpu.make_async_remote_copy(
            src_ref=src, dst_ref=dst, send_sem=send_sem.at[n], recv_sem=recv,
            device_id={"job": job, "seq": seq}, device_id_type=MESH,
        )
        copy.start()
        pending.append(copy)

    def arrive(ref, sem):
        pltpu.make_async_copy(ref, ref, sem).wait()

    barrier = pltpu.get_barrier_semaphore()

    def greet(job, seq):
        pl.semaphore_signal(barrier, inc=1, device_id={"job": job, "seq": seq}, device_id_type=MESH)

    @pl.loop(1, NJ)
    def _(i):
        greet(lax.rem(me + i, NJ), z)

    greet(me, up)
    greet(me, down)
    greet(me, far)
    greet(twin, far)
    pl.semaphore_wait(barrier, NJ - 1 + 4)

    slabs = (slabs_a, slabs_b)

    def slab_copy(p, i):
        to = lax.rem(me + i, NJ)
        return pltpu.make_async_remote_copy(
            src_ref=cache.at[0, :, p * HALF : (p + 1) * HALF, pl.ds(pl.multiple_of(to * 128, 128), 128)],
            dst_ref=slabs[p].at[pl.ds(2 * me, 2)],
            send_sem=route_send.at[0, p, i], recv_sem=route_recv.at[0, p],
            device_id={"job": to, "seq": z}, device_id_type=MESH,
        )

    my_columns = pl.ds(pl.multiple_of(me * 128, 128), 128)
    own_slab = [
        pltpu.make_async_copy(
            cache.at[0, :, p * HALF : (p + 1) * HALF, my_columns],
            slabs[p].at[pl.ds(2 * me, 2)],
            local_sem.at[p],
        )
        for p in range(2)
    ]
    for p in range(2):

        @pl.loop(1, NJ)
        def _(i):
            slab_copy(p, i).start()

        own_slab[p].start()

    weights = ((w_text, wt), (w_key, wk), (w_value, wv))
    keeps = [
        pltpu.make_async_copy(shard, whole.at[0, me], start_recv.at[t, 0])
        for t, (shard, whole) in enumerate(weights)
    ]
    for t, (shard, whole) in enumerate(weights):
        keeps[t].start()
        send(shard, whole.at[1, me], start_recv.at[t, 1], me, far)
    bias[:, 0:HB] = jnp.broadcast_to(b_text[...].reshape(1, HB).astype(jnp.float32), (16, HB)).astype(jnp.bfloat16)
    bias[:, HB : HB + KB] = jnp.broadcast_to(b_value[...].reshape(1, KB).astype(jnp.float32), (16, KB)).astype(jnp.bfloat16)
    send(bias, bias_far, bias_recv.at[0], me, far)
    fetch = [
        pltpu.make_async_copy(query.at[0, :, pl.ds(b * KB, KB)], qv.at[b], query_sem.at[b])
        for b in range(NZ)
    ]
    for copy in fetch:
        copy.start()

    def piece(t, h, a, b, part=None):
        ref = weights[t][1].at[h, at_uv(a, b) + core]
        if part is None:
            return ref
        n = DEPTHS[t] // 2
        return ref.at[pl.ds(part * n, n)]

    def give(t, h, a, b, da, db, slot, part=None):
        ref = piece(t, h, a, b, part)
        send(ref, ref, flow_recv.at[t, h, slot], at_uv(da, db) + core, z)

    def share(t, h, a, b):
        ref = piece(t, h, a, b)
        send(ref, ref, twin_recv.at[t, h], twin, z)

    def across(t, h, a, index):
        give(t, h, a, 0, 0, 1, 4 + 4 * index)
        give(t, h, a, 0, 0, -1, 5 + 4 * index)
        share(t, h, a, 0)

    PLACES = (0, -1, 1, 2)

    def own(t, h):
        arrive(weights[t][1].at[h, me], start_recv.at[t, h])
        give(t, h, 0, 0, 1, 0, 0)
        give(t, h, 0, 0, -1, 0, 1)
        across(t, h, 0, 0)

    def near(t, h, side):
        index = PLACES.index(side)
        arrive(piece(t, h, side, 0), flow_recv.at[t, h, index - 1])
        give(t, h, side, 0, -side, 0, index + 1, index - 1)
        across(t, h, side, index)

    def far_off(t, h):
        arrive(piece(t, h, 2, 0, 0), flow_recv.at[t, h, 2])
        arrive(piece(t, h, 2, 0, 1), flow_recv.at[t, h, 3])
        across(t, h, 2, 3)

    def second(t, h, index, side):
        a, part = PLACES[index], (1 + side) // 2
        arrive(piece(t, h, a, side), flow_recv.at[t, h, 4 + 4 * index + part])
        give(t, h, a, side, 0, -side, 6 + 4 * index + part, part)
        share(t, h, a, side)

    def last(t, h, index):
        a = PLACES[index]
        arrive(piece(t, h, a, 2, 0), flow_recv.at[t, h, 6 + 4 * index])
        arrive(piece(t, h, a, 2, 1), flow_recv.at[t, h, 7 + 4 * index])
        share(t, h, a, 2)

    def flow_twin(t, h):
        arrive(weights[t][1].at[h, 0 : NJ // 2], twin_recv.at[t, h])

    def first_row(p):
        return 96 + p * HALF

    def job_copy(p, i):
        to = lax.rem(me + i, NJ)
        return pltpu.make_async_remote_copy(
            src_ref=picked.at[p, to], dst_ref=txt.at[first_row(p) : first_row(p) + HALF, my_columns],
            send_sem=route_send.at[1, p, i], recv_sem=route_recv.at[1, p],
            device_id={"job": to, "seq": z}, device_id_type=MESH,
        )

    own_job = [
        pltpu.make_async_copy(
            picked.at[p, me], txt.at[first_row(p) : first_row(p) + HALF, my_columns], local_sem.at[p]
        )
        for p in range(2)
    ]

    def route_on(p):
        own_slab[p].wait()
        arrive(slabs[p].at[pl.ds(0, 2 * (NJ - 1))], route_recv.at[0, p])

        @pl.loop(0, NJ)
        def _(g):
            picked[p, g] = slabs[p][source[g]]

        @pl.loop(1, NJ)
        def _(i):
            job_copy(p, i).start()

        own_job[p].start()

    def lines(p, way, hops):
        at = first_row(p) - way * hops * ROWS
        return txt.at[at : at + HALF]

    def text_on(p):
        own_job[p].wait()
        arrive(picked.at[p, pl.ds(0, NJ - 1)], route_recv.at[1, p])
        for way in (2 * p - 1, 1 - 2 * p):
            send(lines(p, way, 0), lines(p, way, 1), text_recv.at[p, (1 + way) // 2], me, up if way == 1 else down)

    def text_pass(p):
        way = 2 * p - 1
        arrive(lines(p, way, 1), text_recv.at[p, (1 + way) // 2])
        send(lines(p, way, 1), lines(p, way, 2), text_recv.at[p, 2], me, up if way == 1 else down)

    def text_last(p):
        way = 2 * p - 1
        arrive(lines(p, -way, 1), text_recv.at[p, (1 - way) // 2])
        arrive(lines(p, way, 2), text_recv.at[p, 2])

    def chunk(b, k):
        return hid.at[b, k * ROWS : (k + 1) * ROWS]

    def hid_send(b, k, way, hop, h):
        send(chunk(b, k), chunk(b, k - way), hid_recv.at[h, 0 if way == 1 else 1, hop, k], me, up if way == 1 else down)

    def hid_wait(b, k, way, hop, h):
        arrive(chunk(b, k - way), hid_recv.at[h, 0 if way == 1 else 1, hop, k])

    def embed(h):
        if h == 0:
            text_last(0)
            text_last(1)
        else:
            arrive(bias_far, bias_recv.at[0])
        flow_twin(0, h)
        acc[...] = jnp.zeros_like(acc)

        @pl.loop(0, 4)
        def _(i):
            at = pl.ds(pl.multiple_of(i * 1024, 1024), 1024)
            part = wt[h, pl.ds(i * 8, 8)].reshape(1024, HB)
            acc[...] += jnp.dot(txt[:, at], part, preferred_element_type=jnp.float32)

        beside = (bias if h == 0 else bias_far)[0:1, 0:HB].astype(jnp.float32)
        for r in range(4):
            rows = slice(r * ROWS, (r + 1) * ROWS)
            hid[block(h), rows, :] = jax.nn.gelu(acc[rows, :] + beside, approximate=True).astype(jnp.bfloat16)
        for k in (3, 2, 1):
            hid_send(block(h), k, 1, 0, h)
            hid_send(block(h), 3 - k, -1, 0, h)

    def hidden(h, hop, k, way):
        src = (k - hop + 1) if way == 1 else 3 - (k - hop + 1)
        b = lax.rem(block(h) - way * hop + NZ, NZ)
        hid_wait(b, src, way, hop - 1, h)
        if k > hop:
            hid_send(b, src - way, way, hop, h)

    def project(t, h):
        whole, target, sems = ((wk, kall, key_recv), (wv, vall, value_recv))[t - 1]
        flow_twin(t, h)
        acc[:, 0:KB] = jnp.zeros((WIN, KB), jnp.float32)

        @pl.loop(0, NZ)
        def _(b):
            part = whole[h, pl.ds(b * 4, 4)].reshape(HB, KB)
            acc[:, 0:KB] += jnp.dot(hid[b], part, preferred_element_type=jnp.float32)

        total = acc[:, 0:KB]
        if t == 2:
            total = total + (bias if h == 0 else bias_far)[0:1, HB : HB + KB].astype(jnp.float32)
        target[z, h] = total.astype(jnp.bfloat16)
        for way in (0, 1):
            ring_send(target, sems, 0, h, way)

    def ring_send(target, sems, s, h, way):
        if s < (4 if way == h else 3):
            ref = target.at[lax.rem(z + (NZ - s if way == 0 else s), NZ), h]
            send(ref, ref, sems.at[way, s, h], me, up if way == 0 else down)

    def ring(t, s, h, way):
        target, sems = ((kall, key_recv), (vall, value_recv))[t - 1]
        origin = lax.rem(z + (NZ - s if way == 0 else s), NZ)
        arrive(target.at[origin, h], sems.at[way, s - 1, h])
        ring_send(target, sems, s, h, way)

    live = text_len[me]
    scale = HD ** (-0.5)

    def dead(origin):
        at = lax.broadcasted_iota(jnp.int32, (1, WIN), 1) + (ROWS * origin - 96)
        at = jnp.where(at < 0, at + TXT, jnp.where(at >= TXT, at - TXT, at))
        return jnp.where(at < live, jnp.float32(0), jnp.float32(-1e30))

    NT = (((1,), (1,)), ((), ()))

    def weigh(d):
        q = lax.rem(z + d, 4)
        @pl.loop(0, 2)
        def _(n):
            b = lax.rem(q + 4 * n, NZ)
            other = lax.rem(b + 4, NZ)
            off_a, off_b = dead(b), dead(other)
            for i in range(KB // HD):
                cols = slice(i * HD, (i + 1) * HD)
                ahead = qv[b, :, cols]
                sa = lax.dot_general(ahead, kall[b, 0, :, cols], NT, preferred_element_type=jnp.float32) * scale + off_a
                sb = lax.dot_general(ahead, kall[other, 1, :, cols], NT, preferred_element_type=jnp.float32) * scale + off_b
                peak = jnp.maximum(jnp.max(sa, axis=1, keepdims=True), jnp.max(sb, axis=1, keepdims=True))
                ea, eb = jnp.exp(sa - peak), jnp.exp(sb - peak)
                share_of = 1.0 / (jnp.sum(ea, axis=1, keepdims=True) + jnp.sum(eb, axis=1, keepdims=True))
                prob[b, i, :, 0:WIN] = (ea * share_of).astype(jnp.bfloat16)
                prob[b, i, :, WIN:TXT] = (eb * share_of).astype(jnp.bfloat16)

    def mix(d):
        q = lax.rem(z + d, 4)
        @pl.loop(0, 2)
        def _(n):
            b = lax.rem(q + 4 * n, NZ)
            other = lax.rem(b + 4, NZ)
            for i in range(KB // HD):
                cols = slice(i * HD, (i + 1) * HD)
                total = jnp.dot(prob[b, i, :, 0:WIN], vall[b, 0, :, cols], preferred_element_type=jnp.float32)
                total += jnp.dot(prob[b, i, :, WIN:TXT], vall[other, 1, :, cols], preferred_element_type=jnp.float32)
                out[0, :, pl.ds(pl.multiple_of(b * KB + i * HD, HD), HD)] = total.astype(jnp.bfloat16)

    acts = {
        "own": own, "near": near, "far": far_off, "second": second, "last": last, "route_on": route_on,
        "text_on": text_on, "text_pass": text_pass, "embed": embed, "hid": hidden, "project": project,
        "ring": ring, "weigh": weigh, "mix": mix,
    }
    for name, *where in STEPS:
        if name == "weigh" and where[0] == 2:
            for copy in fetch:
                copy.wait()
        acts[name](*where)

    for copy in pending:
        copy.wait_send()
    for p in range(2):

        @pl.loop(1, NJ)
        def _(i):
            slab_copy(p, i).wait_send()
            job_copy(p, i).wait_send()


def body(text_cache, source, text_len, query, w_text, b_text, w_key, w_value, b_value):
    bf16, dma = jnp.bfloat16, pltpu.SemaphoreType.DMA
    whole, smem, vmem = (pl.BlockSpec(memory_space=s) for s in (pl.ANY, pltpu.SMEM, pltpu.VMEM))
    return pl.pallas_call(
        kernel,
        out_shape=pltpu.VMEM((1, VR, HQ), bf16),
        in_specs=[whole, smem, smem, whole, whole, whole, whole, vmem, vmem],
        out_specs=vmem,
        scratch_shapes=[
            pltpu.VMEM((2 * NJ, HALF, 128), bf16),
            pltpu.VMEM((2 * NJ, HALF, 128), bf16),
            pltpu.VMEM((2, NJ, HALF, 128), bf16),
            pltpu.VMEM((WIN, DT), bf16),
            pltpu.VMEM((2, NJ, DT // NJ, HB), bf16),
            pltpu.VMEM((2, NJ, DM // NJ, KB), bf16),
            pltpu.VMEM((2, NJ, DM // NJ, KB), bf16),
            pltpu.VMEM((NZ, WIN, HB), bf16),
            pltpu.VMEM((NZ, 2, WIN, KB), bf16),
            pltpu.VMEM((NZ, 2, WIN, KB), bf16),
            pltpu.VMEM((NZ, KB // HD, VR, TXT), bf16),
            pltpu.VMEM((NZ, VR, KB), bf16),
            pltpu.VMEM((16, HB + KB), bf16),
            pltpu.VMEM((16, HB + KB), bf16),
            pltpu.VMEM((WIN, HB), jnp.float32),
            dma((N_SEND,)),
            dma((2, 2, NJ)),
            dma((2, 2)),
            dma((2,)),
            dma((3, 2)),
            dma((3, 2, 20)),
            dma((3, 2)),
            dma((2, 3)),
            dma((2, 2, 3, 4)),
            dma((2, 4, 2)),
            dma((2, 4, 2)),
            dma((1,)),
            dma((NZ,)),
        ],
        compiler_params=pltpu.CompilerParams(
            collective_id=0, has_side_effects=True, vmem_limit_bytes=56 * 2**20
        ),
    )(text_cache, source, text_len, query, w_text, w_key, w_value, b_text, b_value)


def solution(mesh):
    in_specs = (
        P("job", None, "seq", None),
        P(),
        P(),
        P("job", "seq", None),
        P("job", "seq"),
        P("seq"),
        P("job", "seq"),
        P("job", "seq"),
        P("seq"),
    )
    out_specs = P("job", "seq", None)
    return jax.shard_map(body, mesh=mesh, in_specs=in_specs, out_specs=out_specs, check_vma=False)
```

```python
import functools

import jax
import jax.numpy as jnp
from jax import lax
from jax.experimental import pallas as pl
from jax.experimental.pallas import tpu as pltpu
from jax.sharding import PartitionSpec as P

MESH = pl.DeviceIdType.MESH
HD = 128
NJ, NZ, NX = 32, 8, 4
TXT, DT, DM, HQ, VR = 512, 4096, 5120, 3072, 256
ROWS = TXT // NZ
HB, KB = DM // NZ, HQ // NZ
WIN = 256
DEPTHS = (DT // NJ, DM // NJ, DM // NJ)
HALF = ROWS // 2
N_SEND = 352
SPOT = (2, 0, 1, 3)
STEPS = (
    ("route_on", 0), ("own", 0, 0), ("route_on", 1), ("near", 0, 0, -1), ("near", 0, 0, 1), ("text_on", 0),
    ("second", 0, 0, 0, -1), ("second", 0, 0, 0, 1), ("text_pass", 0, 0), ("own", 0, 1), ("text_pass", 0, 1),
    ("second", 0, 0, 1, 1), ("text_on", 1), ("far", 0, 0), ("second", 0, 0, 1, -1), ("second", 0, 0, 2, 1),
    ("second", 0, 0, 2, -1), ("last", 0, 0, 0), ("text_pass", 1, 0), ("near", 0, 1, 1), ("near", 0, 1, -1),
    ("second", 0, 1, 0, 1), ("second", 0, 1, 0, -1), ("text_pass", 1, 1), ("second", 0, 0, 3, -1),
    ("second", 0, 0, 3, 1), ("last", 0, 0, 1), ("last", 0, 0, 2), ("second", 0, 1, 2, -1),
    ("second", 0, 1, 2, 1), ("far", 0, 1), ("second", 0, 1, 1, 1), ("second", 0, 1, 1, -1), ("last", 0, 1, 0),
    ("own", 1, 0), ("last", 0, 0, 3), ("last", 0, 1, 2), ("own", 1, 1), ("embed", 0), ("second", 0, 1, 3, -1),
    ("second", 0, 1, 3, 1), ("last", 0, 1, 1), ("near", 1, 0, -1), ("near", 1, 0, 1), ("second", 1, 0, 0, 1),
    ("second", 1, 0, 0, -1), ("near", 1, 1, 1), ("near", 1, 1, -1), ("second", 1, 1, 0, 1),
    ("second", 1, 1, 0, -1), ("hid", 0, 1, 3, 1), ("hid", 0, 1, 3, -1), ("last", 0, 1, 3),
    ("hid", 0, 1, 2, 1), ("hid", 0, 1, 2, -1), ("second", 1, 0, 1, 1), ("far", 1, 0), ("second", 1, 0, 1, -1),
    ("embed", 1), ("hid", 0, 2, 3, 1), ("hid", 0, 2, 3, -1), ("hid", 0, 1, 1, 1), ("hid", 0, 1, 1, -1),
    ("second", 1, 0, 2, -1), ("second", 1, 0, 2, 1), ("last", 1, 0, 0), ("second", 1, 1, 2, -1),
    ("second", 1, 1, 2, 1), ("far", 1, 1), ("hid", 0, 2, 2, 1), ("hid", 0, 2, 2, -1), ("second", 1, 1, 1, 1),
    ("second", 1, 1, 1, -1), ("last", 1, 1, 0), ("hid", 1, 1, 3, 1), ("hid", 1, 1, 3, -1), ("own", 2, 0),
    ("second", 1, 0, 3, -1), ("second", 1, 0, 3, 1), ("last", 1, 0, 1), ("last", 1, 0, 2),
    ("hid", 1, 1, 2, 1), ("hid", 1, 1, 2, -1), ("last", 1, 1, 2), ("own", 2, 1), ("hid", 1, 1, 1, 1),
    ("hid", 1, 1, 1, -1), ("second", 1, 1, 3, -1), ("second", 1, 1, 3, 1), ("last", 1, 1, 1),
    ("hid", 0, 3, 3, 1), ("hid", 0, 3, 3, -1), ("near", 2, 0, 1), ("near", 2, 0, -1), ("second", 2, 0, 0, 1),
    ("second", 2, 0, 0, -1), ("hid", 1, 2, 3, 1), ("hid", 1, 2, 3, -1), ("last", 1, 0, 3),
    ("hid", 1, 2, 2, 1), ("near", 2, 1, 1), ("hid", 1, 2, 2, -1), ("near", 2, 1, -1), ("project", 1, 0, 0),
    ("hid", 1, 3, 3, 1), ("hid", 1, 3, 3, -1), ("project", 1, 0, 1), ("last", 1, 1, 3),
    ("second", 2, 0, 2, -1), ("far", 2, 0), ("second", 2, 0, 2, 1), ("second", 2, 1, 0, -1),
    ("second", 2, 1, 0, 1), ("second", 2, 0, 1, 1), ("second", 2, 0, 1, -1), ("last", 2, 0, 0),
    ("project", 1, 1, 0), ("project", 1, 1, 1), ("ring", 1, 1, 0, 0, 0), ("ring", 1, 1, 0, 1, 0),
    ("ring", 1, 1, 0, 0, 1), ("ring", 1, 1, 0, 1, 1), ("far", 2, 1), ("second", 2, 1, 1, -1),
    ("second", 2, 1, 1, 1), ("second", 2, 1, 2, -1), ("second", 2, 1, 2, 1), ("second", 2, 0, 3, 1),
    ("last", 2, 0, 2), ("second", 2, 0, 3, -1), ("ring", 1, 1, 1, 0, 0), ("ring", 1, 1, 1, 1, 0),
    ("last", 2, 1, 0), ("last", 2, 0, 1), ("ring", 1, 1, 1, 0, 1), ("ring", 1, 1, 1, 1, 1),
    ("second", 2, 1, 3, 1), ("second", 2, 1, 3, -1), ("last", 2, 1, 1), ("last", 2, 1, 2),
    ("ring", 1, 2, 0, 0, 0), ("ring", 1, 2, 0, 1, 0), ("last", 2, 0, 3), ("last", 2, 1, 3),
    ("ring", 1, 2, 0, 0, 1), ("ring", 1, 2, 0, 1, 1), ("project", 2, 0), ("ring", 1, 2, 1, 0, 0),
    ("ring", 1, 2, 1, 1, 0), ("project", 2, 1), ("ring", 1, 2, 1, 0, 1), ("ring", 1, 2, 1, 1, 1),
    ("weigh", 2), ("ring", 1, 3, 0, 0, 0), ("ring", 1, 3, 0, 1, 0), ("ring", 1, 3, 0, 0, 1),
    ("ring", 1, 3, 0, 1, 1), ("ring", 2, 1, 0, 0), ("ring", 2, 1, 0, 1), ("ring", 1, 3, 1, 0, 0),
    ("ring", 1, 3, 1, 1, 0), ("ring", 2, 1, 1, 0), ("ring", 2, 1, 1, 1), ("ring", 1, 3, 1, 0, 1),
    ("weigh", 1), ("ring", 1, 3, 1, 1, 1), ("ring", 1, 4, 0, 0, 0), ("weigh", 3), ("ring", 2, 2, 0, 1),
    ("ring", 1, 4, 0, 0, 1), ("ring", 1, 4, 1, 1, 0), ("ring", 2, 2, 0, 0), ("ring", 2, 2, 1, 1),
    ("ring", 2, 2, 1, 0), ("ring", 1, 4, 1, 1, 1), ("mix", 2), ("weigh", 0), ("ring", 2, 3, 0, 0),
    ("ring", 2, 3, 0, 1), ("ring", 2, 3, 1, 0), ("mix", 1), ("ring", 2, 3, 1, 1), ("mix", 3),
    ("ring", 2, 4, 0, 0), ("ring", 2, 4, 1, 1), ("mix", 0),
)


def kernel(
    cache, source, text_len, query, w_text, w_key, w_value, b_text, b_value, out,
    slabs_a, slabs_b, picked, txt, wt, wk, wv, hid, kall, vall, prob, qv, bias, bias_far, acc,
    send_sem, route_send, route_recv, local_sem, start_recv, flow_recv, twin_recv,
    text_recv, hid_recv, key_recv, value_recv, bias_recv, query_sem,
):
    me, z = lax.axis_index("job"), lax.axis_index("seq")
    core, chip = lax.rem(me, 2), me // 2
    x, y = chip // NX, lax.rem(chip, NX)
    u, v = jnp.where(core == 0, x, y), jnp.where(core == 0, y, x)
    step_u, step_v = 8 - 6 * core, 2 + 6 * core
    up, down, far = lax.rem(z + 1, NZ), lax.rem(z + NZ - 1, NZ), lax.rem(z + 4, NZ)
    twin = me + 1 - 2 * core

    def block(h):
        return z if h == 0 else far

    def at_uv(a, b):
        return lax.rem(u + a + NX, NX) * step_u + lax.rem(v + b + NX, NX) * step_v

    pending = []

    def send(src, dst, recv, job, seq):
        n = len(pending)
        copy = pltpu.make_async_remote_copy(
            src_ref=src, dst_ref=dst, send_sem=send_sem.at[n], recv_sem=recv,
            device_id={"job": job, "seq": seq}, device_id_type=MESH,
        )
        copy.start()
        pending.append(copy)

    def arrive(ref, sem):
        pltpu.make_async_copy(ref, ref, sem).wait()

    barrier = pltpu.get_barrier_semaphore()

    def greet(job, seq):
        pl.semaphore_signal(barrier, inc=1, device_id={"job": job, "seq": seq}, device_id_type=MESH)

    @pl.loop(1, NJ)
    def _(i):
        greet(lax.rem(me + i, NJ), z)

    greet(me, up)
    greet(me, down)
    greet(me, far)
    greet(twin, far)
    pl.semaphore_wait(barrier, NJ - 1 + 4)

    slabs = (slabs_a, slabs_b)

    def slab_copy(p, i):
        to = lax.rem(me + i, NJ)
        return pltpu.make_async_remote_copy(
            src_ref=cache.at[0, :, p * HALF : (p + 1) * HALF, pl.ds(pl.multiple_of(to * 128, 128), 128)],
            dst_ref=slabs[p].at[pl.ds(2 * me, 2)],
            send_sem=route_send.at[0, p, i], recv_sem=route_recv.at[0, p],
            device_id={"job": to, "seq": z}, device_id_type=MESH,
        )

    my_columns = pl.ds(pl.multiple_of(me * 128, 128), 128)
    own_slab = [
        pltpu.make_async_copy(
            cache.at[0, :, p * HALF : (p + 1) * HALF, my_columns],
            slabs[p].at[pl.ds(2 * me, 2)],
            local_sem.at[p],
        )
        for p in range(2)
    ]
    for p in range(2):

        @pl.loop(1, NJ)
        def _(i):
            slab_copy(p, i).start()

        own_slab[p].start()

    weights = ((w_text, wt), (w_key, wk), (w_value, wv))
    keeps = [
        pltpu.make_async_copy(shard, whole.at[0, me], start_recv.at[t, 0])
        for t, (shard, whole) in enumerate(weights)
    ]
    for t, (shard, whole) in enumerate(weights):
        keeps[t].start()
        send(shard, whole.at[1, me], start_recv.at[t, 1], me, far)
    bias[:, 0:HB] = jnp.broadcast_to(b_text[...].reshape(1, HB).astype(jnp.float32), (16, HB)).astype(jnp.bfloat16)
    bias[:, HB : HB + KB] = jnp.broadcast_to(b_value[...].reshape(1, KB).astype(jnp.float32), (16, KB)).astype(jnp.bfloat16)
    send(bias, bias_far, bias_recv.at[0], me, far)
    fetch = [
        pltpu.make_async_copy(query.at[0, :, pl.ds(b * KB, KB)], qv.at[b], query_sem.at[b])
        for b in range(NZ)
    ]
    for copy in fetch:
        copy.start()

    def piece(t, h, a, b, part=None):
        ref = weights[t][1].at[h, at_uv(a, b) + core]
        if part is None:
            return ref
        n = DEPTHS[t] // 2
        return ref.at[pl.ds(part * n, n)]

    def give(t, h, a, b, da, db, slot, part=None):
        ref = piece(t, h, a, b, part)
        send(ref, ref, flow_recv.at[t, h, slot], at_uv(da, db) + core, z)

    def share(t, h, a, b):
        ref = piece(t, h, a, b)
        send(ref, ref, twin_recv.at[t, h], twin, z)

    def across(t, h, a, index):
        give(t, h, a, 0, 0, 1, 4 + 4 * index)
        give(t, h, a, 0, 0, -1, 5 + 4 * index)
        share(t, h, a, 0)

    PLACES = (0, -1, 1, 2)

    def own(t, h):
        arrive(weights[t][1].at[h, me], start_recv.at[t, h])
        give(t, h, 0, 0, 1, 0, 0)
        give(t, h, 0, 0, -1, 0, 1)
        across(t, h, 0, 0)

    def near(t, h, side):
        index = PLACES.index(side)
        arrive(piece(t, h, side, 0), flow_recv.at[t, h, index - 1])
        give(t, h, side, 0, -side, 0, index + 1, index - 1)
        across(t, h, side, index)

    def far_off(t, h):
        arrive(piece(t, h, 2, 0, 0), flow_recv.at[t, h, 2])
        arrive(piece(t, h, 2, 0, 1), flow_recv.at[t, h, 3])
        across(t, h, 2, 3)

    def second(t, h, index, side):
        a, part = PLACES[index], (1 + side) // 2
        arrive(piece(t, h, a, side), flow_recv.at[t, h, 4 + 4 * index + part])
        give(t, h, a, side, 0, -side, 6 + 4 * index + part, part)
        share(t, h, a, side)

    def last(t, h, index):
        a = PLACES[index]
        arrive(piece(t, h, a, 2, 0), flow_recv.at[t, h, 6 + 4 * index])
        arrive(piece(t, h, a, 2, 1), flow_recv.at[t, h, 7 + 4 * index])
        share(t, h, a, 2)

    def flow_twin(t, h):
        arrive(weights[t][1].at[h, 0 : NJ // 2], twin_recv.at[t, h])

    def first_row(p):
        return 96 + p * HALF

    def job_copy(p, i):
        to = lax.rem(me + i, NJ)
        return pltpu.make_async_remote_copy(
            src_ref=picked.at[p, to], dst_ref=txt.at[first_row(p) : first_row(p) + HALF, my_columns],
            send_sem=route_send.at[1, p, i], recv_sem=route_recv.at[1, p],
            device_id={"job": to, "seq": z}, device_id_type=MESH,
        )

    own_job = [
        pltpu.make_async_copy(
            picked.at[p, me], txt.at[first_row(p) : first_row(p) + HALF, my_columns], local_sem.at[p]
        )
        for p in range(2)
    ]

    def route_on(p):
        own_slab[p].wait()
        arrive(slabs[p].at[pl.ds(0, 2 * (NJ - 1))], route_recv.at[0, p])

        @pl.loop(0, NJ)
        def _(g):
            picked[p, g] = slabs[p][source[g]]

        @pl.loop(1, NJ)
        def _(i):
            job_copy(p, i).start()

        own_job[p].start()

    def lines(p, way, hops, side):
        at = first_row(p) - way * hops * ROWS
        return txt.at[at : at + HALF, side * (DT // 2) : (side + 1) * (DT // 2)]

    def text_send(p, way, hops, side):
        to, sem = up if way == 1 else down, text_recv.at[p, (1 + way) // 2 if hops == 0 else 2, side]
        send(lines(p, way, hops, side), lines(p, way, hops + 1, side), sem, me, to)

    def text_on(p):
        own_job[p].wait()
        arrive(picked.at[p, pl.ds(0, NJ - 1)], route_recv.at[1, p])
        for way in (2 * p - 1, 1 - 2 * p):
            for side in range(2):
                text_send(p, way, 0, side)

    def text_pass(p, side):
        way = 2 * p - 1
        arrive(lines(p, way, 1, side), text_recv.at[p, (1 + way) // 2, side])
        text_send(p, way, 1, side)

    def text_last(p):
        way = 2 * p - 1
        for side in range(2):
            arrive(lines(p, -way, 1, side), text_recv.at[p, (1 - way) // 2, side])
            arrive(lines(p, way, 2, side), text_recv.at[p, 2, side])

    def chunk(b, k):
        return hid.at[b, SPOT[k] * ROWS : (SPOT[k] + 1) * ROWS]

    def hid_send(b, k, way, hop, h):
        send(chunk(b, k), chunk(b, k - way), hid_recv.at[h, 0 if way == 1 else 1, hop, k], me, up if way == 1 else down)

    def hid_wait(b, k, way, hop, h):
        arrive(chunk(b, k - way), hid_recv.at[h, 0 if way == 1 else 1, hop, k])

    def embed(h):
        if h == 0:
            text_last(0)
            text_last(1)
        else:
            arrive(bias_far, bias_recv.at[0])
        flow_twin(0, h)
        acc[...] = jnp.zeros_like(acc)

        @pl.loop(0, 4)
        def _(i):
            at = pl.ds(pl.multiple_of(i * 1024, 1024), 1024)
            part = wt[h, pl.ds(i * 8, 8)].reshape(1024, HB)
            acc[...] += jnp.dot(txt[:, at], part, preferred_element_type=jnp.float32)

        beside = (bias if h == 0 else bias_far)[0:1, 0:HB].astype(jnp.float32)
        for r in range(4):
            rows = slice(r * ROWS, (r + 1) * ROWS)
            chunk(block(h), r)[...] = jax.nn.gelu(acc[rows, :] + beside, approximate=True).astype(jnp.bfloat16)
        for k in (3, 2, 1):
            hid_send(block(h), k, 1, 0, h)
            hid_send(block(h), 3 - k, -1, 0, h)

    def hidden(h, hop, k, way):
        src = (k - hop + 1) if way == 1 else 3 - (k - hop + 1)
        b = lax.rem(block(h) - way * hop + NZ, NZ)
        hid_wait(b, src, way, hop - 1, h)
        if k > hop:
            hid_send(b, src - way, way, hop, h)

    def matmul(whole, h, rows):
        acc[rows, 0:KB] = jnp.zeros((rows.stop - rows.start, KB), jnp.float32)

        @pl.loop(0, NZ)
        def _(b):
            part = whole[h, pl.ds(b * 4, 4)].reshape(HB, KB)
            acc[rows, 0:KB] += jnp.dot(hid[b, rows, :], part, preferred_element_type=jnp.float32)

        return acc[rows, 0:KB]

    def half(part):
        return slice(part * (WIN // 2), (part + 1) * (WIN // 2))

    def project(t, h, part=None):
        if not part:
            flow_twin(t, h)
        if t == 1:
            kall[z, h, half(part), :] = matmul(wk, h, half(part)).astype(jnp.bfloat16)
        else:
            total = matmul(wv, h, slice(0, WIN))
            total = total + (bias if h == 0 else bias_far)[0:1, HB : HB + KB].astype(jnp.float32)
            vall[z, h] = total.astype(jnp.bfloat16)
        for way in (0, 1):
            ring_send(t, 0, h, way, part)

    def ring_piece(t, s, h, way, part):
        origin = lax.rem(z + (NZ - s if way == 0 else s), NZ)
        return kall.at[origin, h, half(part)] if t == 1 else vall.at[origin, h]

    def ring_sem(t, s, h, way, part):
        return key_recv.at[way, s, h, part] if t == 1 else value_recv.at[way, s, h]

    def ring_send(t, s, h, way, part):
        if s < (4 if way == h else 3):
            ref = ring_piece(t, s, h, way, part)
            send(ref, ref, ring_sem(t, s, h, way, part), me, up if way == 0 else down)

    def ring(t, s, h, way, part=None):
        arrive(ring_piece(t, s, h, way, part), ring_sem(t, s - 1, h, way, part))
        ring_send(t, s, h, way, part)

    live = text_len[me]
    scale = HD ** (-0.5)

    def dead(origin):
        at = lax.broadcasted_iota(jnp.int32, (1, WIN), 1)
        at = jnp.where(at < 2 * ROWS, at + ROWS, jnp.where(at < 3 * ROWS, at - 2 * ROWS, at))
        at = at + (ROWS * origin - 96)
        at = jnp.where(at < 0, at + TXT, jnp.where(at >= TXT, at - TXT, at))
        return jnp.where(at < live, jnp.float32(0), jnp.float32(-1e30))

    NT = (((1,), (1,)), ((), ()))

    def weigh(d):
        q = lax.rem(z + d, 4)
        @pl.loop(0, 2)
        def _(n):
            b = lax.rem(q + 4 * n, NZ)
            other = lax.rem(b + 4, NZ)
            off_a, off_b = dead(b), dead(other)
            for i in range(KB // HD):
                cols = slice(i * HD, (i + 1) * HD)
                ahead = qv[b, :, cols]
                sa = lax.dot_general(ahead, kall[b, 0, :, cols], NT, preferred_element_type=jnp.float32) * scale + off_a
                sb = lax.dot_general(ahead, kall[other, 1, :, cols], NT, preferred_element_type=jnp.float32) * scale + off_b
                peak = jnp.maximum(jnp.max(sa, axis=1, keepdims=True), jnp.max(sb, axis=1, keepdims=True))
                ea, eb = jnp.exp(sa - peak), jnp.exp(sb - peak)
                share_of = 1.0 / (jnp.sum(ea, axis=1, keepdims=True) + jnp.sum(eb, axis=1, keepdims=True))
                prob[b, i, :, 0:WIN] = (ea * share_of).astype(jnp.bfloat16)
                prob[b, i, :, WIN:TXT] = (eb * share_of).astype(jnp.bfloat16)

    def mix(d):
        q = lax.rem(z + d, 4)
        @pl.loop(0, 2)
        def _(n):
            b = lax.rem(q + 4 * n, NZ)
            other = lax.rem(b + 4, NZ)
            for i in range(KB // HD):
                cols = slice(i * HD, (i + 1) * HD)
                total = jnp.dot(prob[b, i, :, 0:WIN], vall[b, 0, :, cols], preferred_element_type=jnp.float32)
                total += jnp.dot(prob[b, i, :, WIN:TXT], vall[other, 1, :, cols], preferred_element_type=jnp.float32)
                out[0, :, pl.ds(pl.multiple_of(b * KB + i * HD, HD), HD)] = total.astype(jnp.bfloat16)

    def drain(count):
        for copy in pending[:count]:
            copy.wait_send()
        for p in range(2):

            @pl.loop(1, NJ)
            def _(i):
                slab_copy(p, i).wait_send()
                job_copy(p, i).wait_send()

    acts = {
        "own": own, "near": near, "far": far_off, "second": second, "last": last, "route_on": route_on,
        "text_on": text_on, "text_pass": text_pass, "embed": embed, "hid": hidden, "project": project,
        "ring": ring, "weigh": weigh, "mix": mix,
    }
    for name, *where in STEPS:
        if name == "weigh" and where[0] == 2:
            for copy in fetch:
                copy.wait()
        if (name, *where) == ("ring", 2, 4, 0, 0):
            drain(early)
            drained = early
        acts[name](*where)
        if (name, *where) == ("project", 2, 1):
            early = len(pending)


    for copy in pending[drained:]:
        copy.wait_send()


def body(text_cache, source, text_len, query, w_text, b_text, w_key, w_value, b_value):
    bf16, dma = jnp.bfloat16, pltpu.SemaphoreType.DMA
    whole, smem, vmem = (pl.BlockSpec(memory_space=s) for s in (pl.ANY, pltpu.SMEM, pltpu.VMEM))
    return pl.pallas_call(
        kernel,
        out_shape=pltpu.VMEM((1, VR, HQ), bf16),
        in_specs=[whole, smem, smem, whole, whole, whole, whole, vmem, vmem],
        out_specs=vmem,
        scratch_shapes=[
            pltpu.VMEM((2 * NJ, HALF, 128), bf16),
            pltpu.VMEM((2 * NJ, HALF, 128), bf16),
            pltpu.VMEM((2, NJ, HALF, 128), bf16),
            pltpu.VMEM((WIN, DT), bf16),
            pltpu.VMEM((2, NJ, DT // NJ, HB), bf16),
            pltpu.VMEM((2, NJ, DM // NJ, KB), bf16),
            pltpu.VMEM((2, NJ, DM // NJ, KB), bf16),
            pltpu.VMEM((NZ, WIN, HB), bf16),
            pltpu.VMEM((NZ, 2, WIN, KB), bf16),
            pltpu.VMEM((NZ, 2, WIN, KB), bf16),
            pltpu.VMEM((NZ, KB // HD, VR, TXT), bf16),
            pltpu.VMEM((NZ, VR, KB), bf16),
            pltpu.VMEM((16, HB + KB), bf16),
            pltpu.VMEM((16, HB + KB), bf16),
            pltpu.VMEM((WIN, HB), jnp.float32),
            dma((N_SEND,)),
            dma((2, 2, NJ)),
            dma((2, 2)),
            dma((2,)),
            dma((3, 2)),
            dma((3, 2, 20)),
            dma((3, 2)),
            dma((2, 3, 2)),
            dma((2, 2, 3, 4)),
            dma((2, 4, 2, 2)),
            dma((2, 4, 2)),
            dma((1,)),
            dma((NZ,)),
        ],
        compiler_params=pltpu.CompilerParams(
            collective_id=0, has_side_effects=True, vmem_limit_bytes=56 * 2**20
        ),
    )(text_cache, source, text_len, query, w_text, w_key, w_value, b_text, b_value)


def solution(mesh):
    in_specs = (
        P("job", None, "seq", None),
        P(),
        P(),
        P("job", "seq", None),
        P("job", "seq"),
        P("seq"),
        P("job", "seq"),
        P("job", "seq"),
        P("seq"),
    )
    out_specs = P("job", "seq", None)
    return jax.shard_map(body, mesh=mesh, in_specs=in_specs, out_specs=out_specs, check_vma=False)
```

```python
import functools

import jax
import jax.numpy as jnp
from jax import lax
from jax.experimental import pallas as pl
from jax.experimental.pallas import tpu as pltpu
from jax.sharding import PartitionSpec as P

MESH = pl.DeviceIdType.MESH
HD = 128
NJ, NZ, NX = 32, 8, 4
TXT, DT, DM, HQ, VR = 512, 4096, 5120, 3072, 256
ROWS = TXT // NZ
HB, KB = DM // NZ, HQ // NZ
WIN = 256
DEPTHS = (DT // NJ, DM // NJ, DM // NJ)
HALF = ROWS // 2
N_SEND = 352
SPOT = (2, 0, 1, 3)
STEPS = (
    ("own", 0, 0), ("route_on", 0), ("near", 0, 0, -1), ("near", 0, 0, 1), ("route_on", 1),
    ("second", 0, 0, 0, -1), ("second", 0, 0, 0, 1), ("second", 0, 0, 1, 1), ("text_on", 0),
    ("second", 0, 0, 1, -1), ("far", 0, 0), ("own", 0, 1), ("second", 0, 0, 2, -1), ("second", 0, 0, 2, 1),
    ("text_pass", 0, 0), ("text_pass", 0, 1), ("last", 0, 0, 0), ("last", 0, 0, 1), ("text_on", 1),
    ("second", 0, 0, 3, -1), ("second", 0, 0, 3, 1), ("near", 0, 1, -1), ("near", 0, 1, 1),
    ("text_pass", 1, 0), ("second", 0, 1, 0, -1), ("second", 0, 1, 0, 1), ("last", 0, 0, 2),
    ("last", 0, 0, 3), ("text_pass", 1, 1), ("second", 0, 1, 1, 1), ("second", 0, 1, 1, -1), ("far", 0, 1),
    ("own", 1, 0), ("second", 0, 1, 2, -1), ("second", 0, 1, 2, 1), ("last", 0, 1, 0), ("last", 0, 1, 1),
    ("embed", 0), ("second", 0, 1, 3, -1), ("second", 0, 1, 3, 1), ("near", 1, 0, -1), ("near", 1, 0, 1),
    ("second", 1, 0, 0, -1), ("second", 1, 0, 0, 1), ("last", 0, 1, 2), ("last", 0, 1, 3), ("own", 1, 1),
    ("hid", 0, 1, 3, 1), ("hid", 0, 1, 3, -1), ("second", 1, 0, 1, 1), ("second", 1, 0, 1, -1), ("far", 1, 0),
    ("hid", 0, 1, 2, 1), ("hid", 0, 1, 2, -1), ("embed", 1), ("hid", 0, 1, 1, 1), ("hid", 0, 1, 1, -1),
    ("second", 1, 0, 2, -1), ("second", 1, 0, 2, 1), ("last", 1, 0, 0), ("near", 1, 1, -1),
    ("hid", 0, 2, 3, 1), ("hid", 0, 2, 3, -1), ("near", 1, 1, 1), ("second", 1, 1, 0, -1),
    ("second", 1, 1, 0, 1), ("last", 1, 0, 1), ("hid", 0, 2, 2, 1), ("hid", 0, 2, 2, -1),
    ("second", 1, 0, 3, -1), ("second", 1, 0, 3, 1), ("last", 1, 0, 2), ("hid", 1, 1, 3, 1),
    ("hid", 1, 1, 3, -1), ("own", 2, 0), ("second", 1, 1, 1, 1), ("hid", 1, 1, 2, 1), ("hid", 1, 1, 2, -1),
    ("second", 1, 1, 1, -1), ("far", 1, 1), ("second", 1, 1, 2, -1), ("second", 1, 1, 2, 1),
    ("hid", 1, 1, 1, 1), ("hid", 1, 1, 1, -1), ("last", 1, 1, 0), ("last", 1, 0, 3), ("hid", 0, 3, 3, 1),
    ("hid", 0, 3, 3, -1), ("near", 2, 0, -1), ("near", 2, 0, 1), ("hid", 1, 2, 3, 1), ("hid", 1, 2, 3, -1),
    ("second", 2, 0, 0, -1), ("second", 2, 0, 0, 1), ("last", 1, 1, 1), ("hid", 1, 2, 2, 1),
    ("hid", 1, 2, 2, -1), ("project", 1, 0, 0), ("last", 1, 1, 2), ("second", 1, 1, 3, -1),
    ("second", 1, 1, 3, 1), ("hid", 1, 3, 3, 1), ("hid", 1, 3, 3, -1), ("project", 1, 0, 1), ("far", 2, 0),
    ("second", 2, 0, 1, -1), ("second", 2, 0, 1, 1), ("own", 2, 1), ("second", 2, 0, 2, -1),
    ("second", 2, 0, 2, 1), ("last", 2, 0, 0), ("ring", 1, 1, 0, 0, 0), ("ring", 1, 1, 0, 1, 0),
    ("last", 1, 1, 3), ("second", 2, 0, 3, -1), ("second", 2, 0, 3, 1), ("ring", 1, 1, 0, 0, 1),
    ("ring", 1, 1, 0, 1, 1), ("last", 2, 0, 1), ("project", 1, 1, 0), ("project", 1, 1, 1),
    ("ring", 1, 2, 0, 0, 0), ("ring", 1, 2, 0, 1, 0), ("second", 2, 1, 0, -1), ("last", 2, 0, 2),
    ("second", 2, 1, 0, 1), ("near", 2, 1, -1), ("near", 2, 1, 1), ("last", 2, 0, 3), ("ring", 1, 2, 0, 0, 1),
    ("ring", 1, 2, 0, 1, 1), ("last", 2, 1, 0), ("ring", 1, 1, 1, 0, 0), ("ring", 1, 1, 1, 1, 0),
    ("project", 2, 0), ("ring", 1, 1, 1, 0, 1), ("ring", 1, 1, 1, 1, 1), ("second", 2, 1, 1, -1),
    ("second", 2, 1, 1, 1), ("second", 2, 1, 2, -1), ("second", 2, 1, 2, 1), ("far", 2, 1),
    ("ring", 1, 3, 0, 0, 0), ("ring", 1, 3, 0, 1, 0), ("last", 2, 1, 1), ("ring", 1, 3, 0, 0, 1),
    ("ring", 1, 3, 0, 1, 1), ("last", 2, 1, 2), ("second", 2, 1, 3, -1), ("second", 2, 1, 3, 1),
    ("ring", 1, 2, 1, 0, 0), ("ring", 1, 2, 1, 1, 0), ("last", 2, 1, 3), ("ring", 2, 1, 0, 0),
    ("ring", 2, 1, 0, 1), ("project", 2, 1), ("ring", 1, 2, 1, 0, 1), ("ring", 1, 2, 1, 1, 1), ("weigh", 2),
    ("ring", 1, 3, 1, 1, 0), ("ring", 1, 4, 0, 0, 0), ("ring", 1, 4, 0, 0, 1), ("ring", 1, 3, 1, 0, 0),
    ("ring", 2, 2, 0, 1), ("ring", 2, 2, 0, 0), ("ring", 2, 1, 1, 1), ("ring", 1, 3, 1, 1, 1), ("weigh", 3),
    ("ring", 2, 1, 1, 0), ("ring", 1, 4, 1, 1, 0), ("ring", 1, 3, 1, 0, 1), ("weigh", 1),
    ("ring", 2, 3, 0, 1), ("ring", 2, 3, 0, 0), ("ring", 2, 2, 1, 1), ("ring", 2, 2, 1, 0),
    ("ring", 1, 4, 1, 1, 1), ("mix", 2), ("weigh", 0), ("ring", 2, 4, 0, 0), ("ring", 2, 3, 1, 1), ("mix", 3),
    ("ring", 2, 3, 1, 0), ("mix", 1), ("ring", 2, 4, 1, 1), ("mix", 0),
)


def kernel(
    cache, source, text_len, query, w_text, w_key, w_value, b_text, b_value, out,
    slabs_a, slabs_b, picked, txt, wt, wk, wv, hid, kall, vall, prob, qv, bias, bias_far, acc,
    send_sem, route_send, route_recv, local_sem, start_recv, flow_recv, twin_recv,
    text_recv, hid_recv, key_recv, value_recv, bias_recv, query_sem,
):
    me, z = lax.axis_index("job"), lax.axis_index("seq")
    core, chip = lax.rem(me, 2), me // 2
    x, y = chip // NX, lax.rem(chip, NX)
    u, v = jnp.where(core == 0, x, y), jnp.where(core == 0, y, x)
    step_u, step_v = 8 - 6 * core, 2 + 6 * core
    up, down, far = lax.rem(z + 1, NZ), lax.rem(z + NZ - 1, NZ), lax.rem(z + 4, NZ)
    twin = me + 1 - 2 * core

    def block(h):
        return z if h == 0 else far

    def at_uv(a, b):
        return lax.rem(u + a + NX, NX) * step_u + lax.rem(v + b + NX, NX) * step_v

    pending = []

    def send(src, dst, recv, job, seq):
        n = len(pending)
        copy = pltpu.make_async_remote_copy(
            src_ref=src, dst_ref=dst, send_sem=send_sem.at[n], recv_sem=recv,
            device_id={"job": job, "seq": seq}, device_id_type=MESH,
        )
        copy.start()
        pending.append(copy)

    def arrive(ref, sem):
        pltpu.make_async_copy(ref, ref, sem).wait()

    barrier = pltpu.get_barrier_semaphore()

    def greet(job, seq):
        pl.semaphore_signal(barrier, inc=1, device_id={"job": job, "seq": seq}, device_id_type=MESH)

    @pl.loop(1, NJ)
    def _(i):
        greet(lax.rem(me + i, NJ), z)

    greet(me, up)
    greet(me, down)
    greet(me, far)
    greet(twin, far)
    pl.semaphore_wait(barrier, NJ - 1 + 4)

    slabs = (slabs_a, slabs_b)

    def slab_copy(p, i):
        to = lax.rem(me + i, NJ)
        return pltpu.make_async_remote_copy(
            src_ref=cache.at[0, :, p * HALF : (p + 1) * HALF, pl.ds(pl.multiple_of(to * 128, 128), 128)],
            dst_ref=slabs[p].at[pl.ds(2 * me, 2)],
            send_sem=route_send.at[0, p, i], recv_sem=route_recv.at[0, p],
            device_id={"job": to, "seq": z}, device_id_type=MESH,
        )

    my_columns = pl.ds(pl.multiple_of(me * 128, 128), 128)
    own_slab = [
        pltpu.make_async_copy(
            cache.at[0, :, p * HALF : (p + 1) * HALF, my_columns],
            slabs[p].at[pl.ds(2 * me, 2)],
            local_sem.at[p],
        )
        for p in range(2)
    ]
    for p in range(2):

        @pl.loop(1, NJ)
        def _(i):
            slab_copy(p, i).start()

        own_slab[p].start()

    weights = ((w_text, wt), (w_key, wk), (w_value, wv))
    keeps = [
        pltpu.make_async_copy(shard, whole.at[0, me], start_recv.at[t, 0])
        for t, (shard, whole) in enumerate(weights)
    ]
    for t, (shard, whole) in enumerate(weights):
        keeps[t].start()
        send(shard, whole.at[1, me], start_recv.at[t, 1], me, far)
    bias[:, 0:HB] = jnp.broadcast_to(b_text[...].reshape(1, HB).astype(jnp.float32), (16, HB)).astype(jnp.bfloat16)
    bias[:, HB : HB + KB] = jnp.broadcast_to(b_value[...].reshape(1, KB).astype(jnp.float32), (16, KB)).astype(jnp.bfloat16)
    send(bias, bias_far, bias_recv.at[0], me, far)
    fetch = [
        pltpu.make_async_copy(query.at[0, :, pl.ds(b * KB, KB)], qv.at[b], query_sem.at[b])
        for b in range(NZ)
    ]
    for copy in fetch:
        copy.start()

    def piece(t, h, a, b, part=None):
        ref = weights[t][1].at[h, at_uv(a, b) + core]
        if part is None:
            return ref
        n = DEPTHS[t] // 2
        return ref.at[pl.ds(part * n, n)]

    def give(t, h, a, b, da, db, slot, part=None):
        ref = piece(t, h, a, b, part)
        send(ref, ref, flow_recv.at[t, h, slot], at_uv(da, db) + core, z)

    def share(t, h, a, b):
        ref = piece(t, h, a, b)
        send(ref, ref, twin_recv.at[t, h], twin, z)

    def across(t, h, a, index):
        give(t, h, a, 0, 0, 1, 4 + 4 * index)
        give(t, h, a, 0, 0, -1, 5 + 4 * index)
        share(t, h, a, 0)

    PLACES = (0, -1, 1, 2)

    def own(t, h):
        arrive(weights[t][1].at[h, me], start_recv.at[t, h])
        give(t, h, 0, 0, 1, 0, 0)
        give(t, h, 0, 0, -1, 0, 1)
        across(t, h, 0, 0)

    def near(t, h, side):
        index = PLACES.index(side)
        arrive(piece(t, h, side, 0), flow_recv.at[t, h, index - 1])
        give(t, h, side, 0, -side, 0, index + 1, index - 1)
        across(t, h, side, index)

    def far_off(t, h):
        arrive(piece(t, h, 2, 0, 0), flow_recv.at[t, h, 2])
        arrive(piece(t, h, 2, 0, 1), flow_recv.at[t, h, 3])
        across(t, h, 2, 3)

    def second(t, h, index, side):
        a, part = PLACES[index], (1 + side) // 2
        arrive(piece(t, h, a, side), flow_recv.at[t, h, 4 + 4 * index + part])
        give(t, h, a, side, 0, -side, 6 + 4 * index + part, part)
        share(t, h, a, side)

    def last(t, h, index):
        a = PLACES[index]
        arrive(piece(t, h, a, 2, 0), flow_recv.at[t, h, 6 + 4 * index])
        arrive(piece(t, h, a, 2, 1), flow_recv.at[t, h, 7 + 4 * index])
        share(t, h, a, 2)

    def flow_twin(t, h):
        arrive(weights[t][1].at[h, 0 : NJ // 2], twin_recv.at[t, h])

    def first_row(p):
        return 96 + p * HALF

    def job_copy(p, i):
        to = lax.rem(me + i, NJ)
        return pltpu.make_async_remote_copy(
            src_ref=picked.at[p, to], dst_ref=txt.at[first_row(p) : first_row(p) + HALF, my_columns],
            send_sem=route_send.at[1, p, i], recv_sem=route_recv.at[1, p],
            device_id={"job": to, "seq": z}, device_id_type=MESH,
        )

    own_job = [
        pltpu.make_async_copy(
            picked.at[p, me], txt.at[first_row(p) : first_row(p) + HALF, my_columns], local_sem.at[p]
        )
        for p in range(2)
    ]

    def route_on(p):
        own_slab[p].wait()
        arrive(slabs[p].at[pl.ds(0, 2 * (NJ - 1))], route_recv.at[0, p])

        @pl.loop(0, NJ)
        def _(g):
            picked[p, g] = slabs[p][source[g]]

        @pl.loop(1, NJ)
        def _(i):
            job_copy(p, i).start()

        own_job[p].start()

    def lines(p, way, hops, side):
        at = first_row(p) - way * hops * ROWS
        return txt.at[at : at + HALF, side * (DT // 2) : (side + 1) * (DT // 2)]

    def text_send(p, way, hops, side):
        to, sem = up if way == 1 else down, text_recv.at[p, (1 + way) // 2 if hops == 0 else 2, side]
        send(lines(p, way, hops, side), lines(p, way, hops + 1, side), sem, me, to)

    def text_on(p):
        own_job[p].wait()
        arrive(picked.at[p, pl.ds(0, NJ - 1)], route_recv.at[1, p])
        for way in (2 * p - 1, 1 - 2 * p):
            for side in range(2):
                text_send(p, way, 0, side)

    def text_pass(p, side):
        way = 2 * p - 1
        arrive(lines(p, way, 1, side), text_recv.at[p, (1 + way) // 2, side])
        text_send(p, way, 1, side)

    def text_last(p):
        way = 2 * p - 1
        for side in range(2):
            arrive(lines(p, -way, 1, side), text_recv.at[p, (1 - way) // 2, side])
            arrive(lines(p, way, 2, side), text_recv.at[p, 2, side])

    def chunk(b, k):
        return hid.at[b, SPOT[k] * ROWS : (SPOT[k] + 1) * ROWS]

    def hid_send(b, k, way, hop, h):
        send(chunk(b, k), chunk(b, k - way), hid_recv.at[h, 0 if way == 1 else 1, hop, k], me, up if way == 1 else down)

    def hid_wait(b, k, way, hop, h):
        arrive(chunk(b, k - way), hid_recv.at[h, 0 if way == 1 else 1, hop, k])

    def embed(h):
        if h == 0:
            text_last(0)
            text_last(1)
        else:
            arrive(bias_far, bias_recv.at[0])
        flow_twin(0, h)
        acc[...] = jnp.zeros_like(acc)

        @pl.loop(0, 4)
        def _(i):
            at = pl.ds(pl.multiple_of(i * 1024, 1024), 1024)
            part = wt[h, pl.ds(i * 8, 8)].reshape(1024, HB)
            acc[...] += jnp.dot(txt[:, at], part, preferred_element_type=jnp.float32)

        beside = (bias if h == 0 else bias_far)[0:1, 0:HB].astype(jnp.float32)
        for r in range(4):
            rows = slice(r * ROWS, (r + 1) * ROWS)
            chunk(block(h), r)[...] = jax.nn.gelu(acc[rows, :] + beside, approximate=True).astype(jnp.bfloat16)
        for k in (3, 2, 1):
            hid_send(block(h), k, 1, 0, h)
            hid_send(block(h), 3 - k, -1, 0, h)

    def hidden(h, hop, k, way):
        src = (k - hop + 1) if way == 1 else 3 - (k - hop + 1)
        b = lax.rem(block(h) - way * hop + NZ, NZ)
        hid_wait(b, src, way, hop - 1, h)
        if k > hop:
            hid_send(b, src - way, way, hop, h)

    def matmul(whole, h, rows):
        acc[rows, 0:KB] = jnp.zeros((rows.stop - rows.start, KB), jnp.float32)

        @pl.loop(0, NZ)
        def _(b):
            part = whole[h, pl.ds(b * 4, 4)].reshape(HB, KB)
            acc[rows, 0:KB] += jnp.dot(hid[b, rows, :], part, preferred_element_type=jnp.float32)

        return acc[rows, 0:KB]

    def half(part):
        return slice(part * (WIN // 2), (part + 1) * (WIN // 2))

    def project(t, h, part=None):
        if not part:
            flow_twin(t, h)
        if t == 1:
            kall[z, h, half(part), :] = matmul(wk, h, half(part)).astype(jnp.bfloat16)
        else:
            total = matmul(wv, h, slice(0, WIN))
            total = total + (bias if h == 0 else bias_far)[0:1, HB : HB + KB].astype(jnp.float32)
            vall[z, h] = total.astype(jnp.bfloat16)
        for way in (0, 1):
            ring_send(t, 0, h, way, part)

    def ring_piece(t, s, h, way, part):
        origin = lax.rem(z + (NZ - s if way == 0 else s), NZ)
        return kall.at[origin, h, half(part)] if t == 1 else vall.at[origin, h]

    def ring_sem(t, s, h, way, part):
        return key_recv.at[way, s, h, part] if t == 1 else value_recv.at[way, s, h]

    def ring_send(t, s, h, way, part):
        if s < (4 if way == h else 3):
            ref = ring_piece(t, s, h, way, part)
            send(ref, ref, ring_sem(t, s, h, way, part), me, up if way == 0 else down)

    def ring(t, s, h, way, part=None):
        arrive(ring_piece(t, s, h, way, part), ring_sem(t, s - 1, h, way, part))
        ring_send(t, s, h, way, part)

    live = text_len[me]
    scale = HD ** (-0.5)

    def dead(origin):
        at = lax.broadcasted_iota(jnp.int32, (1, WIN), 1)
        at = jnp.where(at < 2 * ROWS, at + ROWS, jnp.where(at < 3 * ROWS, at - 2 * ROWS, at))
        at = at + (ROWS * origin - 96)
        at = jnp.where(at < 0, at + TXT, jnp.where(at >= TXT, at - TXT, at))
        return jnp.where(at < live, jnp.float32(0), jnp.float32(-1e30))

    NT = (((1,), (1,)), ((), ()))

    def weigh(d):
        q = lax.rem(z + d, 4)
        @pl.loop(0, 2)
        def _(n):
            b = lax.rem(q + 4 * n, NZ)
            other = lax.rem(b + 4, NZ)
            off_a, off_b = dead(b), dead(other)
            for i in range(KB // HD):
                cols = slice(i * HD, (i + 1) * HD)
                ahead = qv[b, :, cols]
                sa = lax.dot_general(ahead, kall[b, 0, :, cols], NT, preferred_element_type=jnp.float32) * scale + off_a
                sb = lax.dot_general(ahead, kall[other, 1, :, cols], NT, preferred_element_type=jnp.float32) * scale + off_b
                peak = jnp.maximum(jnp.max(sa, axis=1, keepdims=True), jnp.max(sb, axis=1, keepdims=True))
                ea, eb = jnp.exp(sa - peak), jnp.exp(sb - peak)
                share_of = 1.0 / (jnp.sum(ea, axis=1, keepdims=True) + jnp.sum(eb, axis=1, keepdims=True))
                prob[b, i, :, 0:WIN] = (ea * share_of).astype(jnp.bfloat16)
                prob[b, i, :, WIN:TXT] = (eb * share_of).astype(jnp.bfloat16)

    def mix(d):
        q = lax.rem(z + d, 4)
        @pl.loop(0, 2)
        def _(n):
            b = lax.rem(q + 4 * n, NZ)
            other = lax.rem(b + 4, NZ)
            for i in range(KB // HD):
                cols = slice(i * HD, (i + 1) * HD)
                total = jnp.dot(prob[b, i, :, 0:WIN], vall[b, 0, :, cols], preferred_element_type=jnp.float32)
                total += jnp.dot(prob[b, i, :, WIN:TXT], vall[other, 1, :, cols], preferred_element_type=jnp.float32)
                out[0, :, pl.ds(pl.multiple_of(b * KB + i * HD, HD), HD)] = total.astype(jnp.bfloat16)

    def drain(count):
        for copy in pending[:count]:
            copy.wait_send()
        for p in range(2):

            @pl.loop(1, NJ)
            def _(i):
                slab_copy(p, i).wait_send()
                job_copy(p, i).wait_send()

    acts = {
        "own": own, "near": near, "far": far_off, "second": second, "last": last, "route_on": route_on,
        "text_on": text_on, "text_pass": text_pass, "embed": embed, "hid": hidden, "project": project,
        "ring": ring, "weigh": weigh, "mix": mix,
    }
    for name, *where in STEPS:
        if name == "weigh" and where[0] == 2:
            for copy in fetch:
                copy.wait()
        if (name, *where) == ("ring", 2, 4, 0, 0):
            drain(early)
            drained = early
        acts[name](*where)
        if (name, *where) == ("project", 2, 1):
            early = len(pending)


    for copy in pending[drained:]:
        copy.wait_send()


def body(text_cache, source, text_len, query, w_text, b_text, w_key, w_value, b_value):
    bf16, dma = jnp.bfloat16, pltpu.SemaphoreType.DMA
    whole, smem, vmem = (pl.BlockSpec(memory_space=s) for s in (pl.ANY, pltpu.SMEM, pltpu.VMEM))
    return pl.pallas_call(
        kernel,
        out_shape=pltpu.VMEM((1, VR, HQ), bf16),
        in_specs=[whole, smem, smem, whole, whole, whole, whole, vmem, vmem],
        out_specs=vmem,
        scratch_shapes=[
            pltpu.VMEM((2 * NJ, HALF, 128), bf16),
            pltpu.VMEM((2 * NJ, HALF, 128), bf16),
            pltpu.VMEM((2, NJ, HALF, 128), bf16),
            pltpu.VMEM((WIN, DT), bf16),
            pltpu.VMEM((2, NJ, DT // NJ, HB), bf16),
            pltpu.VMEM((2, NJ, DM // NJ, KB), bf16),
            pltpu.VMEM((2, NJ, DM // NJ, KB), bf16),
            pltpu.VMEM((NZ, WIN, HB), bf16),
            pltpu.VMEM((NZ, 2, WIN, KB), bf16),
            pltpu.VMEM((NZ, 2, WIN, KB), bf16),
            pltpu.VMEM((NZ, KB // HD, VR, TXT), bf16),
            pltpu.VMEM((NZ, VR, KB), bf16),
            pltpu.VMEM((16, HB + KB), bf16),
            pltpu.VMEM((16, HB + KB), bf16),
            pltpu.VMEM((WIN, HB), jnp.float32),
            dma((N_SEND,)),
            dma((2, 2, NJ)),
            dma((2, 2)),
            dma((2,)),
            dma((3, 2)),
            dma((3, 2, 20)),
            dma((3, 2)),
            dma((2, 3, 2)),
            dma((2, 2, 3, 4)),
            dma((2, 4, 2, 2)),
            dma((2, 4, 2)),
            dma((1,)),
            dma((NZ,)),
        ],
        compiler_params=pltpu.CompilerParams(
            collective_id=0, has_side_effects=True, vmem_limit_bytes=56 * 2**20
        ),
    )(text_cache, source, text_len, query, w_text, w_key, w_value, b_text, b_value)


def solution(mesh):
    in_specs = (
        P("job", None, "seq", None),
        P(),
        P(),
        P("job", "seq", None),
        P("job", "seq"),
        P("seq"),
        P("job", "seq"),
        P("job", "seq"),
        P("seq"),
    )
    out_specs = P("job", "seq", None)
    return jax.shard_map(body, mesh=mesh, in_specs=in_specs, out_specs=out_specs, check_vma=False)
```

```python
import functools

import jax
import jax.numpy as jnp
from jax import lax
from jax.experimental import pallas as pl
from jax.experimental.pallas import tpu as pltpu
from jax.sharding import PartitionSpec as P

MESH = pl.DeviceIdType.MESH
HD = 128
NJ, NZ, NX = 32, 8, 4
TXT, DT, DM, HQ, VR = 512, 4096, 5120, 3072, 256
ROWS = TXT // NZ
HB, KB = DM // NZ, HQ // NZ
WIN = 256
DEPTHS = (DT // NJ, DM // NJ, DM // NJ)
HALF = ROWS // 2
N_SEND = 352
SPOT = (2, 0, 1, 3)
STEPS = (
    ("own", 0, 0), ("route_on", 0), ("near", 0, 0, -1), ("near", 0, 0, 1), ("route_on", 1),
    ("second", 0, 0, 0, -1), ("second", 0, 0, 0, 1), ("second", 0, 0, 1, 1), ("text_on", 0),
    ("second", 0, 0, 1, -1), ("far", 0, 0), ("own", 0, 1), ("second", 0, 0, 2, -1), ("second", 0, 0, 2, 1),
    ("text_pass", 0, 0), ("text_pass", 0, 1), ("last", 0, 0, 0), ("last", 0, 0, 1), ("text_on", 1),
    ("second", 0, 0, 3, -1), ("second", 0, 0, 3, 1), ("near", 0, 1, -1), ("near", 0, 1, 1),
    ("text_pass", 1, 0), ("second", 0, 1, 0, -1), ("second", 0, 1, 0, 1), ("last", 0, 0, 2),
    ("last", 0, 0, 3), ("text_pass", 1, 1), ("second", 0, 1, 1, 1), ("second", 0, 1, 1, -1), ("far", 0, 1),
    ("own", 1, 0), ("second", 0, 1, 2, -1), ("second", 0, 1, 2, 1), ("last", 0, 1, 0), ("last", 0, 1, 1),
    ("embed", 0), ("second", 0, 1, 3, -1), ("second", 0, 1, 3, 1), ("near", 1, 0, -1), ("near", 1, 0, 1),
    ("second", 1, 0, 0, -1), ("second", 1, 0, 0, 1), ("last", 0, 1, 2), ("last", 0, 1, 3), ("own", 1, 1),
    ("hid", 0, 1, 3, 1), ("hid", 0, 1, 3, -1), ("second", 1, 0, 1, 1), ("second", 1, 0, 1, -1), ("far", 1, 0),
    ("hid", 0, 1, 2, 1), ("hid", 0, 1, 2, -1), ("embed", 1), ("hid", 0, 1, 1, 1), ("hid", 0, 1, 1, -1),
    ("second", 1, 0, 2, -1), ("second", 1, 0, 2, 1), ("last", 1, 0, 0), ("near", 1, 1, -1),
    ("hid", 0, 2, 3, 1), ("hid", 0, 2, 3, -1), ("near", 1, 1, 1), ("second", 1, 1, 0, -1),
    ("second", 1, 1, 0, 1), ("last", 1, 0, 1), ("hid", 0, 2, 2, 1), ("hid", 0, 2, 2, -1),
    ("second", 1, 0, 3, -1), ("second", 1, 0, 3, 1), ("last", 1, 0, 2), ("hid", 1, 1, 3, 1),
    ("hid", 1, 1, 3, -1), ("own", 2, 0), ("second", 1, 1, 1, 1), ("hid", 1, 1, 2, 1), ("hid", 1, 1, 2, -1),
    ("second", 1, 1, 1, -1), ("far", 1, 1), ("second", 1, 1, 2, -1), ("second", 1, 1, 2, 1),
    ("hid", 1, 1, 1, 1), ("hid", 1, 1, 1, -1), ("last", 1, 1, 0), ("last", 1, 0, 3), ("hid", 0, 3, 3, 1),
    ("hid", 0, 3, 3, -1), ("near", 2, 0, -1), ("near", 2, 0, 1), ("hid", 1, 2, 3, 1), ("hid", 1, 2, 3, -1),
    ("second", 2, 0, 0, -1), ("second", 2, 0, 0, 1), ("last", 1, 1, 1), ("hid", 1, 2, 2, 1),
    ("hid", 1, 2, 2, -1), ("project", 1, 0, 0), ("last", 1, 1, 2), ("second", 1, 1, 3, -1),
    ("second", 1, 1, 3, 1), ("hid", 1, 3, 3, 1), ("hid", 1, 3, 3, -1), ("project", 1, 0, 1), ("far", 2, 0),
    ("second", 2, 0, 1, -1), ("second", 2, 0, 1, 1), ("own", 2, 1), ("second", 2, 0, 2, -1),
    ("second", 2, 0, 2, 1), ("last", 2, 0, 0), ("ring", 1, 1, 0, 0, 0), ("ring", 1, 1, 0, 1, 0),
    ("last", 1, 1, 3), ("second", 2, 0, 3, -1), ("second", 2, 0, 3, 1), ("ring", 1, 1, 0, 0, 1),
    ("ring", 1, 1, 0, 1, 1), ("last", 2, 0, 1), ("project", 1, 1, 0), ("project", 1, 1, 1),
    ("ring", 1, 2, 0, 0, 0), ("ring", 1, 2, 0, 1, 0), ("second", 2, 1, 0, -1), ("last", 2, 0, 2),
    ("second", 2, 1, 0, 1), ("near", 2, 1, -1), ("near", 2, 1, 1), ("last", 2, 0, 3), ("ring", 1, 2, 0, 0, 1),
    ("ring", 1, 2, 0, 1, 1), ("last", 2, 1, 0), ("ring", 1, 1, 1, 0, 0), ("ring", 1, 1, 1, 1, 0),
    ("project", 2, 0), ("ring", 1, 1, 1, 0, 1), ("ring", 1, 1, 1, 1, 1), ("second", 2, 1, 1, -1),
    ("second", 2, 1, 1, 1), ("second", 2, 1, 2, -1), ("second", 2, 1, 2, 1), ("far", 2, 1),
    ("ring", 1, 3, 0, 0, 0), ("ring", 1, 3, 0, 1, 0), ("last", 2, 1, 1), ("ring", 1, 3, 0, 0, 1),
    ("ring", 1, 3, 0, 1, 1), ("last", 2, 1, 2), ("second", 2, 1, 3, -1), ("second", 2, 1, 3, 1),
    ("ring", 1, 2, 1, 0, 0), ("ring", 1, 2, 1, 1, 0), ("last", 2, 1, 3), ("ring", 2, 1, 0, 0),
    ("ring", 2, 1, 0, 1), ("project", 2, 1), ("ring", 1, 2, 1, 0, 1), ("ring", 1, 2, 1, 1, 1), ("weigh", 2),
    ("ring", 1, 3, 1, 1, 0), ("ring", 1, 4, 0, 0, 0), ("ring", 1, 4, 0, 0, 1), ("ring", 1, 3, 1, 0, 0),
    ("ring", 2, 2, 0, 1), ("ring", 2, 2, 0, 0), ("ring", 2, 1, 1, 1), ("ring", 1, 3, 1, 1, 1), ("weigh", 3),
    ("ring", 2, 1, 1, 0), ("ring", 1, 4, 1, 1, 0), ("ring", 1, 3, 1, 0, 1), ("weigh", 1),
    ("ring", 2, 3, 0, 1), ("ring", 2, 3, 0, 0), ("ring", 2, 2, 1, 1), ("ring", 2, 2, 1, 0),
    ("ring", 1, 4, 1, 1, 1), ("mix", 2), ("weigh", 0), ("ring", 2, 4, 0, 0), ("ring", 2, 3, 1, 1), ("mix", 3),
    ("ring", 2, 3, 1, 0), ("mix", 1), ("ring", 2, 4, 1, 1), ("mix", 0),
)


def kernel(
    cache, source, text_len, query, w_text, w_key, w_value, b_text, b_value, out,
    slabs_a, slabs_b, picked, txt, wt, wk, wv, hid, kall, vall, prob, qv, bias, bias_far, acc,
    send_sem, route_send, route_recv, local_sem, start_recv, flow_recv, twin_recv,
    text_recv, hid_recv, key_recv, value_recv, bias_recv, query_sem,
):
    me, z = lax.axis_index("job"), lax.axis_index("seq")
    core, chip = lax.rem(me, 2), me // 2
    x, y = chip // NX, lax.rem(chip, NX)
    u, v = jnp.where(core == 0, x, y), jnp.where(core == 0, y, x)
    step_u, step_v = 8 - 6 * core, 2 + 6 * core
    up, down, far = lax.rem(z + 1, NZ), lax.rem(z + NZ - 1, NZ), lax.rem(z + 4, NZ)
    twin = me + 1 - 2 * core

    def block(h):
        return z if h == 0 else far

    def at_uv(a, b):
        return lax.rem(u + a + NX, NX) * step_u + lax.rem(v + b + NX, NX) * step_v

    pending = []

    def send(src, dst, recv, job, seq):
        n = len(pending)
        copy = pltpu.make_async_remote_copy(
            src_ref=src, dst_ref=dst, send_sem=send_sem.at[n], recv_sem=recv,
            device_id={"job": job, "seq": seq}, device_id_type=MESH,
        )
        copy.start()
        pending.append(copy)

    def arrive(ref, sem):
        pltpu.make_async_copy(ref, ref, sem).wait()

    barrier = pltpu.get_barrier_semaphore()

    def greet(job, seq):
        pl.semaphore_signal(barrier, inc=1, device_id={"job": job, "seq": seq}, device_id_type=MESH)

    @pl.loop(1, NJ)
    def _(i):
        greet(lax.rem(me + i, NJ), z)

    greet(me, up)
    greet(me, down)
    greet(me, far)
    greet(twin, far)
    pl.semaphore_wait(barrier, NJ - 1 + 4)

    slabs = (slabs_a, slabs_b)

    def slab_copy(p, i):
        to = lax.rem(me + i, NJ)
        return pltpu.make_async_remote_copy(
            src_ref=cache.at[0, :, p * HALF : (p + 1) * HALF, pl.ds(pl.multiple_of(to * 128, 128), 128)],
            dst_ref=slabs[p].at[pl.ds(2 * me, 2)],
            send_sem=route_send.at[0, p, i], recv_sem=route_recv.at[0, p],
            device_id={"job": to, "seq": z}, device_id_type=MESH,
        )

    my_columns = pl.ds(pl.multiple_of(me * 128, 128), 128)
    own_slab = [
        pltpu.make_async_copy(
            cache.at[0, :, p * HALF : (p + 1) * HALF, my_columns],
            slabs[p].at[pl.ds(2 * me, 2)],
            local_sem.at[p],
        )
        for p in range(2)
    ]
    for p in range(2):

        @pl.loop(1, NJ)
        def _(i):
            slab_copy(p, i).start()

        own_slab[p].start()

    weights = ((w_text, wt), (w_key, wk), (w_value, wv))
    keeps = [
        pltpu.make_async_copy(shard, whole.at[0, me], start_recv.at[t, 0])
        for t, (shard, whole) in enumerate(weights)
    ]
    for t, (shard, whole) in enumerate(weights):
        keeps[t].start()
        send(shard, whole.at[1, me], start_recv.at[t, 1], me, far)
    bias[:, 0:HB] = jnp.broadcast_to(b_text[...].reshape(1, HB).astype(jnp.float32), (16, HB)).astype(jnp.bfloat16)
    bias[:, HB : HB + KB] = jnp.broadcast_to(b_value[...].reshape(1, KB).astype(jnp.float32), (16, KB)).astype(jnp.bfloat16)
    send(bias, bias_far, bias_recv.at[0], me, far)
    fetch = [
        pltpu.make_async_copy(query.at[0, :, pl.ds(b * KB, KB)], qv.at[b], query_sem.at[b])
        for b in range(NZ)
    ]
    for copy in fetch:
        copy.start()

    def piece(t, h, a, b, part=None):
        ref = weights[t][1].at[h, at_uv(a, b) + core]
        if part is None:
            return ref
        n = DEPTHS[t] // 2
        return ref.at[pl.ds(part * n, n)]

    def give(t, h, a, b, da, db, slot, part=None):
        ref = piece(t, h, a, b, part)
        send(ref, ref, flow_recv.at[t, h, slot], at_uv(da, db) + core, z)

    def share(t, h, a, b):
        ref = piece(t, h, a, b)
        send(ref, ref, twin_recv.at[t, h], twin, z)

    def across(t, h, a, index):
        give(t, h, a, 0, 0, 1, 4 + 4 * index)
        give(t, h, a, 0, 0, -1, 5 + 4 * index)
        share(t, h, a, 0)

    PLACES = (0, -1, 1, 2)

    def own(t, h):
        arrive(weights[t][1].at[h, me], start_recv.at[t, h])
        give(t, h, 0, 0, 1, 0, 0)
        give(t, h, 0, 0, -1, 0, 1)
        across(t, h, 0, 0)

    def near(t, h, side):
        index = PLACES.index(side)
        arrive(piece(t, h, side, 0), flow_recv.at[t, h, index - 1])
        give(t, h, side, 0, -side, 0, index + 1, index - 1)
        across(t, h, side, index)

    def far_off(t, h):
        arrive(piece(t, h, 2, 0, 0), flow_recv.at[t, h, 2])
        arrive(piece(t, h, 2, 0, 1), flow_recv.at[t, h, 3])
        across(t, h, 2, 3)

    def second(t, h, index, side):
        a, part = PLACES[index], (1 + side) // 2
        arrive(piece(t, h, a, side), flow_recv.at[t, h, 4 + 4 * index + part])
        give(t, h, a, side, 0, -side, 6 + 4 * index + part, part)
        share(t, h, a, side)

    def last(t, h, index):
        a = PLACES[index]
        arrive(piece(t, h, a, 2, 0), flow_recv.at[t, h, 6 + 4 * index])
        arrive(piece(t, h, a, 2, 1), flow_recv.at[t, h, 7 + 4 * index])
        share(t, h, a, 2)

    def flow_twin(t, h):
        arrive(weights[t][1].at[h, 0 : NJ // 2], twin_recv.at[t, h])

    def first_row(p):
        return 96 + p * HALF

    def job_copy(p, i):
        to = lax.rem(me + i, NJ)
        return pltpu.make_async_remote_copy(
            src_ref=picked.at[p, to], dst_ref=txt.at[first_row(p) : first_row(p) + HALF, my_columns],
            send_sem=route_send.at[1, p, i], recv_sem=route_recv.at[1, p],
            device_id={"job": to, "seq": z}, device_id_type=MESH,
        )

    own_job = [
        pltpu.make_async_copy(
            picked.at[p, me], txt.at[first_row(p) : first_row(p) + HALF, my_columns], local_sem.at[p]
        )
        for p in range(2)
    ]

    def route_on(p):
        own_slab[p].wait()
        arrive(slabs[p].at[pl.ds(0, 2 * (NJ - 1))], route_recv.at[0, p])

        @pl.loop(0, NJ)
        def _(g):
            picked[p, g] = slabs[p][source[g]]

        @pl.loop(1, NJ)
        def _(i):
            job_copy(p, i).start()

        own_job[p].start()

    def lines(p, way, hops, side):
        at = first_row(p) - way * hops * ROWS
        return txt.at[at : at + HALF, side * (DT // 2) : (side + 1) * (DT // 2)]

    def text_send(p, way, hops, side):
        to, sem = up if way == 1 else down, text_recv.at[p, (1 + way) // 2 if hops == 0 else 2, side]
        send(lines(p, way, hops, side), lines(p, way, hops + 1, side), sem, me, to)

    def text_on(p):
        own_job[p].wait()
        arrive(picked.at[p, pl.ds(0, NJ - 1)], route_recv.at[1, p])
        for way in (2 * p - 1, 1 - 2 * p):
            for side in range(2):
                text_send(p, way, 0, side)

    def text_pass(p, side):
        way = 2 * p - 1
        arrive(lines(p, way, 1, side), text_recv.at[p, (1 + way) // 2, side])
        text_send(p, way, 1, side)

    def text_last(p):
        way = 2 * p - 1
        for side in range(2):
            arrive(lines(p, -way, 1, side), text_recv.at[p, (1 - way) // 2, side])
            arrive(lines(p, way, 2, side), text_recv.at[p, 2, side])

    def chunk(b, k):
        return hid.at[b, SPOT[k] * ROWS : (SPOT[k] + 1) * ROWS]

    def hid_send(b, k, way, hop, h):
        send(chunk(b, k), chunk(b, k - way), hid_recv.at[h, 0 if way == 1 else 1, hop, k], me, up if way == 1 else down)

    def hid_wait(b, k, way, hop, h):
        arrive(chunk(b, k - way), hid_recv.at[h, 0 if way == 1 else 1, hop, k])

    def embed(h):
        if h == 0:
            text_last(0)
            text_last(1)
        else:
            arrive(bias_far, bias_recv.at[0])
        flow_twin(0, h)
        acc[...] = jnp.zeros_like(acc)

        @pl.loop(0, 2)
        def _(i):
            at = pl.ds(pl.multiple_of(i * 2048, 2048), 2048)
            part = wt[h, pl.ds(i * 16, 16)].reshape(2048, HB)
            acc[...] += jnp.dot(txt[:, at], part, preferred_element_type=jnp.float32)

        beside = (bias if h == 0 else bias_far)[0:1, 0:HB].astype(jnp.float32)
        for r in range(4):
            rows = slice(r * ROWS, (r + 1) * ROWS)
            chunk(block(h), r)[...] = jax.nn.gelu(acc[rows, :] + beside, approximate=True).astype(jnp.bfloat16)
        for k in (3, 2, 1):
            hid_send(block(h), k, 1, 0, h)
            hid_send(block(h), 3 - k, -1, 0, h)

    def hidden(h, hop, k, way):
        src = (k - hop + 1) if way == 1 else 3 - (k - hop + 1)
        b = lax.rem(block(h) - way * hop + NZ, NZ)
        hid_wait(b, src, way, hop - 1, h)
        if k > hop:
            hid_send(b, src - way, way, hop, h)

    def matmul(whole, h, rows):
        acc[rows, 0:KB] = jnp.zeros((rows.stop - rows.start, KB), jnp.float32)

        @pl.loop(0, NZ // 2)
        def _(b):
            part = whole[h, pl.ds(b * 8, 8)].reshape(2 * HB, KB)
            pair = jnp.concatenate([hid[2 * b, rows, :], hid[2 * b + 1, rows, :]], axis=1)
            acc[rows, 0:KB] += jnp.dot(pair, part, preferred_element_type=jnp.float32)

        return acc[rows, 0:KB]

    def half(part):
        return slice(part * (WIN // 2), (part + 1) * (WIN // 2))

    def project(t, h, part=None):
        if not part:
            flow_twin(t, h)
        if t == 1:
            kall[z, h, half(part), :] = matmul(wk, h, half(part)).astype(jnp.bfloat16)
        else:
            total = matmul(wv, h, slice(0, WIN))
            total = total + (bias if h == 0 else bias_far)[0:1, HB : HB + KB].astype(jnp.float32)
            vall[z, h] = total.astype(jnp.bfloat16)
        for way in (0, 1):
            ring_send(t, 0, h, way, part)

    def ring_piece(t, s, h, way, part):
        origin = lax.rem(z + (NZ - s if way == 0 else s), NZ)
        return kall.at[origin, h, half(part)] if t == 1 else vall.at[origin, h]

    def ring_sem(t, s, h, way, part):
        return key_recv.at[way, s, h, part] if t == 1 else value_recv.at[way, s, h]

    def ring_send(t, s, h, way, part):
        if s < (4 if way == h else 3):
            ref = ring_piece(t, s, h, way, part)
            send(ref, ref, ring_sem(t, s, h, way, part), me, up if way == 0 else down)

    def ring(t, s, h, way, part=None):
        arrive(ring_piece(t, s, h, way, part), ring_sem(t, s - 1, h, way, part))
        ring_send(t, s, h, way, part)

    live = text_len[me]
    scale = HD ** (-0.5)

    def dead(origin):
        at = lax.broadcasted_iota(jnp.int32, (1, WIN), 1)
        at = jnp.where(at < 2 * ROWS, at + ROWS, jnp.where(at < 3 * ROWS, at - 2 * ROWS, at))
        at = at + (ROWS * origin - 96)
        at = jnp.where(at < 0, at + TXT, jnp.where(at >= TXT, at - TXT, at))
        return jnp.where(at < live, jnp.float32(0), jnp.float32(-1e30))

    NT = (((1,), (1,)), ((), ()))

    def weigh(d):
        q = lax.rem(z + d, 4)
        @pl.loop(0, 2)
        def _(n):
            b = lax.rem(q + 4 * n, NZ)
            other = lax.rem(b + 4, NZ)
            off_a, off_b = dead(b), dead(other)
            for i in range(KB // HD):
                cols = slice(i * HD, (i + 1) * HD)
                ahead = qv[b, :, cols]
                sa = lax.dot_general(ahead, kall[b, 0, :, cols], NT, preferred_element_type=jnp.float32) * scale + off_a
                sb = lax.dot_general(ahead, kall[other, 1, :, cols], NT, preferred_element_type=jnp.float32) * scale + off_b
                peak = jnp.maximum(jnp.max(sa, axis=1, keepdims=True), jnp.max(sb, axis=1, keepdims=True))
                ea, eb = jnp.exp(sa - peak), jnp.exp(sb - peak)
                share_of = 1.0 / (jnp.sum(ea, axis=1, keepdims=True) + jnp.sum(eb, axis=1, keepdims=True))
                prob[b, i, :, 0:WIN] = (ea * share_of).astype(jnp.bfloat16)
                prob[b, i, :, WIN:TXT] = (eb * share_of).astype(jnp.bfloat16)

    def mix(d):
        q = lax.rem(z + d, 4)
        @pl.loop(0, 2)
        def _(n):
            b = lax.rem(q + 4 * n, NZ)
            other = lax.rem(b + 4, NZ)
            for i in range(KB // HD):
                cols = slice(i * HD, (i + 1) * HD)
                total = jnp.dot(prob[b, i, :, 0:WIN], vall[b, 0, :, cols], preferred_element_type=jnp.float32)
                total += jnp.dot(prob[b, i, :, WIN:TXT], vall[other, 1, :, cols], preferred_element_type=jnp.float32)
                out[0, :, pl.ds(pl.multiple_of(b * KB + i * HD, HD), HD)] = total.astype(jnp.bfloat16)

    def drain(count):
        for copy in pending[:count]:
            copy.wait_send()
        for p in range(2):

            @pl.loop(1, NJ)
            def _(i):
                slab_copy(p, i).wait_send()
                job_copy(p, i).wait_send()

    acts = {
        "own": own, "near": near, "far": far_off, "second": second, "last": last, "route_on": route_on,
        "text_on": text_on, "text_pass": text_pass, "embed": embed, "hid": hidden, "project": project,
        "ring": ring, "weigh": weigh, "mix": mix,
    }
    for name, *where in STEPS:
        if name == "weigh" and where[0] == 2:
            for copy in fetch:
                copy.wait()
        if (name, *where) == ("ring", 2, 4, 0, 0):
            drain(early)
            drained = early
        acts[name](*where)
        if (name, *where) == ("project", 2, 1):
            early = len(pending)


    for copy in pending[drained:]:
        copy.wait_send()


def body(text_cache, source, text_len, query, w_text, b_text, w_key, w_value, b_value):
    bf16, dma = jnp.bfloat16, pltpu.SemaphoreType.DMA
    whole, smem, vmem = (pl.BlockSpec(memory_space=s) for s in (pl.ANY, pltpu.SMEM, pltpu.VMEM))
    return pl.pallas_call(
        kernel,
        out_shape=pltpu.VMEM((1, VR, HQ), bf16),
        in_specs=[whole, smem, smem, whole, whole, whole, whole, vmem, vmem],
        out_specs=vmem,
        scratch_shapes=[
            pltpu.VMEM((2 * NJ, HALF, 128), bf16),
            pltpu.VMEM((2 * NJ, HALF, 128), bf16),
            pltpu.VMEM((2, NJ, HALF, 128), bf16),
            pltpu.VMEM((WIN, DT), bf16),
            pltpu.VMEM((2, NJ, DT // NJ, HB), bf16),
            pltpu.VMEM((2, NJ, DM // NJ, KB), bf16),
            pltpu.VMEM((2, NJ, DM // NJ, KB), bf16),
            pltpu.VMEM((NZ, WIN, HB), bf16),
            pltpu.VMEM((NZ, 2, WIN, KB), bf16),
            pltpu.VMEM((NZ, 2, WIN, KB), bf16),
            pltpu.VMEM((NZ, KB // HD, VR, TXT), bf16),
            pltpu.VMEM((NZ, VR, KB), bf16),
            pltpu.VMEM((16, HB + KB), bf16),
            pltpu.VMEM((16, HB + KB), bf16),
            pltpu.VMEM((WIN, HB), jnp.float32),
            dma((N_SEND,)),
            dma((2, 2, NJ)),
            dma((2, 2)),
            dma((2,)),
            dma((3, 2)),
            dma((3, 2, 20)),
            dma((3, 2)),
            dma((2, 3, 2)),
            dma((2, 2, 3, 4)),
            dma((2, 4, 2, 2)),
            dma((2, 4, 2)),
            dma((1,)),
            dma((NZ,)),
        ],
        compiler_params=pltpu.CompilerParams(
            collective_id=0, has_side_effects=True, vmem_limit_bytes=56 * 2**20
        ),
    )(text_cache, source, text_len, query, w_text, w_key, w_value, b_text, b_value)


def solution(mesh):
    in_specs = (
        P("job", None, "seq", None),
        P(),
        P(),
        P("job", "seq", None),
        P("job", "seq"),
        P("seq"),
        P("job", "seq"),
        P("job", "seq"),
        P("seq"),
    )
    out_specs = P("job", "seq", None)
    return jax.shard_map(body, mesh=mesh, in_specs=in_specs, out_specs=out_specs, check_vma=False)
```
